256 devices in a mesh: dp: 32 (over z, y), seq: 8 (over x, core).
Axes of the slice: x: 4, y: 4, z: 8, core: 2. Of those that a mesh axis runs over, the one named last changes fastest.
Arguments:
- projected: bfloat16 [32, 1024, 9216], P('dp', 'seq'), may hold values from -12 to 12
- cotangent: bfloat16 [32, 1024, 3072], P('dp', 'seq'), may hold values from -6 to 6
- lengths: int32 [32], replicated, may hold values from 64 to 512, as said below
- text_lengths: int32 [32], replicated, may hold values from 128 to 512, as said below
- destinations: int32 [32], replicated, may hold values from 0 to 31, as said below
Outputs:
- attended: bfloat16 [32, 1024, 3072], P('dp', 'seq')
- projected_grad: bfloat16 [32, 1024, 9216], P('dp', 'seq')
The draws below stay inside these ranges and needn't reach their ends.
Inputs may be any that keep to these rules, and one draw needn't show every extreme that they name: `lengths`: live latent tokens are the first slots of a clip; some clip has exactly 512. `text_lengths`: live text tokens are the first of the clip's 512 text slots; some clip has exactly 512. destinations is a permutation of 0..31.
All inputs are finite; a program needn't handle non-finite values.
Results may differ from the reference program's by a relative error of at most 0.005.
Values may be sent and summed in bfloat16 or wider, within the bound.
No kernel may reach another device: no remote copies, remote signals or barrier semaphores. Data moves between devices by JAX's collectives and lax.ppermute only.
A program may use at most 64 MiB of HBM per device.

```python
import math
import jax
import jax.numpy as jnp
from jax import lax

D = 3072
HEADS = 24
HEAD_DIM = 128
CAP = 512
TXT = 512
CL_DEV = 1
SEQ_LEN = 1024
CLIPS = 32


def draw_projected(key, part):
    key = jax.random.fold_in(key, 11)
    first_key, second_key = jax.random.split(key, 2)
    shape = (CLIPS, SEQ_LEN, 3, HEADS, HEAD_DIM)
    spread = jnp.exp(jax.random.uniform(second_key, (CLIPS, SEQ_LEN, 3, HEADS, 1), minval=math.log(0.4), maxval=math.log(4.0)))
    sample = jnp.clip(jax.random.normal(first_key, shape), -3.0, 3.0) * spread
    return sample.reshape(CLIPS, SEQ_LEN, 3 * D).astype(jnp.bfloat16)


def draw_lengths(key, part):
    key = jax.random.fold_in(key, 3)
    first_key, second_key = jax.random.split(key)
    drawn = jax.random.randint(first_key, (CLIPS,), CAP // 8, CAP + 1)
    chosen = jax.random.randint(second_key, (), 0, CLIPS)
    return jnp.where(jnp.arange(CLIPS) == chosen, CAP, drawn).astype(jnp.int32)


def draw_text_lengths(key, part):
    key = jax.random.fold_in(key, 5)
    first_key, second_key = jax.random.split(key)
    drawn = jax.random.randint(first_key, (CLIPS,), TXT // 4, TXT + 1)
    chosen = jax.random.randint(second_key, (), 0, CLIPS)
    return jnp.where(jnp.arange(CLIPS) == chosen, TXT, drawn).astype(jnp.int32)


def draw_destinations(key, part):
    key = jax.random.fold_in(key, 7)
    rank_count = CLIPS // CL_DEV
    orders = jax.vmap(lambda single_key: jax.random.permutation(single_key, rank_count))(jax.random.split(key, CL_DEV))
    return jnp.transpose(orders).reshape(CLIPS).astype(jnp.int32)


def levels(stream_key, dims, cuts, least, largest):
    def one(axis_at, shards_of):
        steps = jax.random.uniform(jax.random.fold_in(jax.random.fold_in(stream_key, 6), axis_at), (shards_of,), jnp.float32, least / len(cuts), largest / len(cuts))
        return jnp.repeat(jnp.exp(steps), dims[axis_at] // shards_of).reshape((-1,) + (1,) * (len(dims) - axis_at - 1))

    level = one(*cuts[0])
    for cut in cuts[1:]:
        level = level * one(*cut)
    return level


def normal_values(own_key, dims, deviation, limit, shards=(), held_as=jnp.bfloat16):
    factor_of = levels(own_key, dims, shards, -0.22, 0.18) if shards else 1.0
    values = jax.random.normal(own_key, dims, jnp.float32) * deviation * factor_of
    return jnp.minimum(jnp.maximum(values, -limit), limit).astype(held_as)


def setup_inputs(seed: int = 0) -> dict:
    seeds = jax.random.split(jax.random.key(seed), 6)
    return {
        "projected": draw_projected(jax.random.fold_in(seeds[5], 71), 0),
        "cotangent": normal_values(seeds[1], (CLIPS, SEQ_LEN, D), 1.0, 6.0, ((0, 32), (1, 8))),
        "lengths": draw_lengths(jax.random.fold_in(seeds[5], 71), 0),
        "text_lengths": draw_text_lengths(jax.random.fold_in(seeds[5], 71), 0),
        "destinations": draw_destinations(jax.random.fold_in(seeds[5], 71), 0),
    }


def head_pass(items):
    queries, key_rows, value_rows, grad_out, live_mask = items
    scaling = HEAD_DIM ** -0.5
    scores = jnp.dot(queries, key_rows.T, precision=lax.Precision.HIGHEST, preferred_element_type=jnp.float32) * scaling
    scores = jnp.where(live_mask[None, :] > 0, scores, -1e30)
    row_top = jnp.max(scores, axis=-1, keepdims=True)
    exponent = jnp.exp(scores - row_top)
    probabilities = exponent / jnp.sum(exponent, axis=-1, keepdims=True)
    prob_half = lax.optimization_barrier(probabilities.astype(jnp.bfloat16)).astype(jnp.float32)
    outputs = jnp.dot(prob_half, value_rows, precision=lax.Precision.HIGHEST, preferred_element_type=jnp.float32) * live_mask[:, None]
    grad_value = jnp.dot(prob_half.T, grad_out, precision=lax.Precision.HIGHEST, preferred_element_type=jnp.float32)
    grad_prob = jnp.dot(grad_out, value_rows.T, precision=lax.Precision.HIGHEST, preferred_element_type=jnp.float32)
    row_dot = jnp.sum(probabilities * grad_prob, axis=-1, keepdims=True)
    grad_scores = lax.optimization_barrier((probabilities * (grad_prob - row_dot)).astype(jnp.bfloat16)).astype(jnp.float32)
    grad_query = jnp.dot(grad_scores, key_rows, precision=lax.Precision.HIGHEST, preferred_element_type=jnp.float32) * scaling
    grad_key = jnp.dot(grad_scores.T, queries, precision=lax.Precision.HIGHEST, preferred_element_type=jnp.float32) * scaling
    return outputs.astype(jnp.bfloat16), jnp.stack([grad_query, grad_key, grad_value], axis=1).astype(jnp.bfloat16)


def clip_pass(block, grad_block, live_mask):
    count = block.shape[0]
    parts = jnp.moveaxis(block.astype(jnp.float32).reshape(count, 3, HEADS, HEAD_DIM), 2, 0)
    grad_out = jnp.moveaxis(grad_block.astype(jnp.float32).reshape(count, HEADS, HEAD_DIM), 1, 0) * live_mask[None, :, None]
    masks = jnp.broadcast_to(live_mask[None, :], (HEADS, count))
    outputs, gradients = lax.map(head_pass, (parts[:, :, 0], parts[:, :, 1], parts[:, :, 2], grad_out, masks))
    outputs = jnp.moveaxis(outputs, 0, 1).reshape(count, D)
    gradients = jnp.moveaxis(gradients, 0, 2).reshape(count, 3 * D)
    return outputs, gradients


def reference(projected, cotangent, lengths, text_lengths, destinations):
    clip_count = projected.shape[0]
    position = jnp.arange(SEQ_LEN, dtype=jnp.int32)[None, :]
    live_mask = ((position < lengths[:, None]) | ((position >= CAP) & (position < CAP + text_lengths[:, None]))).astype(jnp.float32)
    slot_index = jnp.arange(clip_count, dtype=jnp.int32) % CL_DEV
    target = (destinations * CL_DEV + slot_index).astype(jnp.int32)
    incoming = cotangent[target]

    def single(items):
        return clip_pass(items[0], items[1], items[2])

    outputs, gradients = lax.map(single, (projected, incoming, live_mask))
    attended = jnp.zeros_like(outputs).at[target].set(outputs)
    return attended, gradients
```

```python
import functools
import jax
import jax.numpy as jnp
from jax import lax
from jax.experimental import pallas as pl
from jax.experimental.pallas import tpu as pltpu
from jax.sharding import PartitionSpec as P

HEADS = 24
DH = 128
CAP = 512
SEQ = 1024
RANKS = 32
SHARDS = 8
ROWS = SEQ // SHARDS
MINE = HEADS // SHARDS
GRP = MINE * DH
WIDTH = HEADS * DH
CHIPS = SHARDS // 2
CH = 2 * ROWS
SCALE = DH ** -0.5
LOG2E = 1.4426950408889634
NT = (((1,), (1,)), ((), ()))

ANY = pl.BlockSpec(memory_space=pl.ANY)
SMEM = pl.BlockSpec(memory_space=pltpu.SMEM)
BF = jnp.bfloat16
F32 = jnp.float32


def copies(body, count, given, late, cost=4):
    def kernel(*refs):
        sems = refs[-1]
        started = []
        used = refs[:given] + refs[given + late : -1]
        for n, (src, dst) in enumerate(body(*used)):
            cp = pltpu.make_async_copy(src, dst, sems.at[n])
            cp.start()
            started.append(cp)
        for cp in started:
            cp.wait()

    return functools.partial(
        pl.pallas_call,
        kernel,
        scratch_shapes=[pltpu.SemaphoreType.DMA((count,))],
        compiler_params=pltpu.CompilerParams(vmem_limit_bytes=1 << 20),
        cost_estimate=pl.CostEstimate(flops=0, bytes_accessed=cost << 20, transcendentals=0),
    )


def place(at, k):
    return lax.bitwise_and(lax.shift_right_logical(at[0], 1) + k, CHIPS - 1), at[0] & 1


def split_projected(at, projected, *late):
    def body(at_ref, x_ref, own, other):
        for k in range(CHIPS):
            chip, core = place(at_ref, k)
            for out, head in ((own, 2 * chip + core), (other, 2 * chip + 1 - core)):
                for t in range(3):
                    start = pl.multiple_of(t * WIDTH + head * GRP, GRP)
                    yield x_ref.at[:, pl.ds(start, GRP)], out.at[k, :, pl.ds(t * GRP, GRP)]

    return copies(body, 6 * CHIPS, 2, len(late))(
        out_shape=[pltpu.HBM((CHIPS, ROWS, 3 * GRP), BF)] * 2,
        in_specs=[SMEM, ANY] + [ANY] * len(late),
        out_specs=[ANY] * 2,
        name="split_projected",
    )(at, projected, *late)


def join_gradient(at, blocks, sibling, *late):
    def body(at_ref, *refs):
        out = refs[-1]
        for k in range(CHIPS):
            chip, core = place(at_ref, k)
            mine = refs[k].at[pl.ds(0, ROWS)], 2 * chip + core
            for src, head in (mine, (refs[CHIPS].at[k], 2 * chip + 1 - core)):
                for t in range(3):
                    start = pl.multiple_of(t * WIDTH + head * GRP, GRP)
                    yield src.at[:, pl.ds(t * GRP, GRP)], out.at[:, pl.ds(start, GRP)]

    return copies(body, 6 * CHIPS, 2 + CHIPS, len(late))(
        out_shape=jax.ShapeDtypeStruct((ROWS, 3 * WIDTH), BF),
        in_specs=[SMEM] + [ANY] * (1 + CHIPS + len(late)),
        out_specs=ANY,
        name="join_gradient",
    )(at, *blocks, sibling, *late)


def pair(own, recv, *late):
    width = own.shape[2]

    def body(own_ref, recv_ref, *outs):
        for k in range(CHIPS):
            yield own_ref.at[k], outs[k].at[pl.ds(0, ROWS)]
            yield recv_ref.at[k], outs[k].at[pl.ds(ROWS, ROWS)]

    return copies(body, 2 * CHIPS, 2, len(late))(
        out_shape=[jax.ShapeDtypeStruct((2 * ROWS, width), BF)] * CHIPS,
        in_specs=[ANY] * (2 + len(late)),
        out_specs=[ANY] * CHIPS,
        name="pair",
    )(own, recv, *late)


def for_sibling(blocks, *late):
    width = blocks[0].shape[1]

    def body(*refs):
        for k in range(CHIPS):
            yield refs[k].at[pl.ds(ROWS, ROWS)], refs[CHIPS].at[k]

    return copies(body, CHIPS, CHIPS, len(late))(
        out_shape=jax.ShapeDtypeStruct((CHIPS, ROWS, width), BF),
        in_specs=[ANY] * (CHIPS + len(late)),
        out_specs=ANY,
        name="for_sibling",
    )(*blocks, *late)


def to_pieces(rows, *late):
    def body(x_ref, out):
        for a in range(8):
            for b in range(4):
                yield x_ref.at[pl.ds(16 * a, 16), pl.ds(768 * b, 768)], out.at[4 * a + b]

    return copies(body, RANKS, 1, len(late))(
        out_shape=jax.ShapeDtypeStruct((RANKS, 16, 768), BF),
        in_specs=[ANY] + [ANY] * len(late),
        out_specs=ANY,
        name="to_pieces",
    )(rows, *late)


def from_pieces(pieces, *late):
    def body(x_ref, out):
        for a in range(8):
            for b in range(4):
                yield x_ref.at[4 * a + b], out.at[pl.ds(16 * a, 16), pl.ds(768 * b, 768)]

    return copies(body, RANKS, 1, len(late))(
        out_shape=jax.ShapeDtypeStruct((ROWS, WIDTH), BF),
        in_specs=[ANY] + [ANY] * len(late),
        out_specs=ANY,
        name="from_pieces",
    )(pieces, *late)


def reorder(destinations, pieces, back, *late):
    def body(d_ref, x_ref, out):
        for c in range(RANKS):
            if back:
                yield x_ref.at[c], out.at[d_ref[c]]
            else:
                yield x_ref.at[d_ref[c]], out.at[c]

    return copies(body, RANKS, 2, len(late), 100)(
        out_shape=jax.ShapeDtypeStruct((RANKS, 16, 768), BF),
        in_specs=[SMEM, ANY] + [ANY] * len(late),
        out_specs=ANY,
        name="reorder",
    )(destinations, pieces, *late)


def split_cotangent(at, pieces, *late):
    def body(at_ref, x_ref, own, other):
        for k in range(CHIPS):
            chip, core = place(at_ref, k)
            for out, half in ((own, core), (other, 1 - core)):
                start = pl.multiple_of(half * GRP, GRP)
                for a in range(8):
                    src = x_ref.at[4 * a + chip, :, pl.ds(start, GRP)]
                    yield src, out.at[k, pl.ds(16 * a, 16)]

    return copies(body, 16 * CHIPS, 2, len(late))(
        out_shape=[jax.ShapeDtypeStruct((CHIPS, ROWS, GRP), BF)] * 2,
        in_specs=[SMEM, ANY] + [ANY] * len(late),
        out_specs=[ANY] * 2,
        name="split_cotangent",
    )(at, pieces, *late)


def join_pieces(at, blocks, sibling, *late):
    def body(at_ref, *refs):
        out = refs[-1]
        for k in range(CHIPS):
            chip, core = place(at_ref, k)
            for src, half in ((refs[k], core), (refs[CHIPS].at[k], 1 - core)):
                start = pl.multiple_of(half * GRP, GRP)
                for a in range(8):
                    yield src.at[pl.ds(16 * a, 16)], out.at[4 * a + chip, :, pl.ds(start, GRP)]

    return copies(body, 16 * CHIPS, 2 + CHIPS, len(late))(
        out_shape=jax.ShapeDtypeStruct((RANKS, 16, 768), BF),
        in_specs=[SMEM] + [ANY] * (1 + CHIPS + len(late)),
        out_specs=ANY,
        name="join_pieces",
    )(at, *blocks, sibling, *late)


def live_rows(at, lengths, text_lengths):
    row = lax.broadcasted_iota(jnp.int32, (SEQ, DH), 0)
    chip = lax.bitwise_and((at[0] >> 1) + CHIPS - lax.shift_right_logical(row, 8), CHIPS - 1)
    core = lax.bitwise_xor(at[0] & 1, lax.bitwise_and(lax.shift_right_logical(row, 7), 1))
    pos = (2 * chip + core) * ROWS + lax.bitwise_and(row, ROWS - 1)
    latent, text = lengths[at[1]], text_lengths[at[1]]
    return (pos < latent) | ((pos >= CAP) & (pos < CAP + text))


def fetch(srcs, dst, sems):
    started = []
    for k in range(CHIPS):
        cp = pltpu.make_async_copy(srcs[k], dst.at[pl.ds(k * CH, CH)], sems.at[k])
        cp.start()
        started.append(cp)
    for cp in started:
        cp.wait()


def cols(part, head):
    return pl.ds(pl.multiple_of(part * GRP + head * DH, DH), DH)


def forward_kernel(at, lengths, text_lengths, *refs):
    xs = refs[:CHIPS]
    outs = refs[CHIPS : 2 * CHIPS]
    wide, prob, kept, held, sems, kept_sem = refs[2 * CHIPS :]
    g = pl.program_id(0)
    keep = pltpu.make_async_copy(held, kept, kept_sem)

    @pl.when(g == 0)
    def _():
        fetch(xs, held, sems)
        keep.start()

    @pl.when(g == MINE - 1)
    def _():
        keep.wait()

    live = live_rows(at, lengths, text_lengths)
    lane = lax.broadcasted_iota(jnp.int32, (SEQ, DH), 1)
    dead = jnp.where(live | (lane > 0), 0.0, -1e30).astype(BF)
    unit = jnp.where(lane == 0, 1.0, 0.0).astype(BF)
    q = jnp.concatenate([held[:, cols(0, g)], unit], axis=1)
    k = jnp.concatenate([held[:, cols(1, g)], dead], axis=1)
    vt = held[:, cols(2, g)].T
    livef = live.astype(F32)
    for n in range(SEQ // CH):
        part = slice(n * CH, (n + 1) * CH)
        s = lax.dot_general(k, q[part], NT, preferred_element_type=F32)
        top = jnp.max(s, axis=0, keepdims=True)
        e = jnp.exp2((s - top) * (SCALE * LOG2E))
        full = e * (1.0 / jnp.sum(e, axis=0, keepdims=True))
        p = full.astype(BF)
        rest = (full - p.astype(F32)).astype(BF)
        prob[0, :, part] = full
        o = jnp.dot(vt, p, preferred_element_type=F32)
        more = jnp.dot(vt, rest, preferred_element_type=F32)
        wide[part, pl.ds(pl.multiple_of(g * DH, DH), DH)] = (o + more).T
        o = o.T * livef[part]
        outs[n][:, pl.ds(pl.multiple_of(g * DH, DH), DH)] = o.astype(BF)


def backward_kernel(at, lengths, text_lengths, *refs):
    cs = refs[:CHIPS]
    kept, wide, prob = refs[CHIPS : CHIPS + 3]
    outs = refs[CHIPS + 3 : 2 * CHIPS + 3]
    held, cot, dst, pst, sems, kept_sem = refs[2 * CHIPS + 3 :]
    g = pl.program_id(0)

    @pl.when(g == 0)
    def _():
        back = pltpu.make_async_copy(kept, held, kept_sem)
        back.start()
        fetch(cs, cot, sems)
        back.wait()

    live = live_rows(at, lengths, text_lengths)
    lane = lax.broadcasted_iota(jnp.int32, (SEQ, DH), 1)
    mine = pl.ds(pl.multiple_of(g * DH, DH), DH)
    do = jnp.where(live, cot[:, mine], jnp.zeros((), BF))
    dot = jnp.sum(do.astype(F32) * wide[:, mine], axis=1, keepdims=True)
    hi = dot.astype(BF).astype(F32)
    mid = (dot - hi).astype(BF).astype(F32)
    low = dot - hi - mid
    less = jnp.where(lane == 0, -hi, jnp.where(lane == 1, -mid, jnp.where(lane == 2, -low, 0.0)))
    dox = jnp.concatenate([do, less.astype(BF)], axis=1)
    units = jnp.where(lane < 3, 1.0, 0.0).astype(BF)
    vx = jnp.concatenate([held[:, cols(2, g)], units], axis=1)
    kt = held[:, cols(1, g)].T
    for n in range(SEQ // CH):
        part = slice(n * CH, (n + 1) * CH)
        dp = lax.dot_general(vx, dox[part], NT, preferred_element_type=F32)
        p = prob[0, :, part]
        pst[:, part] = p.astype(BF)
        ds = (p * dp).astype(BF)
        dst[:, part] = ds
        dq = jnp.dot(kt, ds, preferred_element_type=F32).T * SCALE
        outs[n][:, cols(0, g)] = dq.astype(BF)
    q = held[:, cols(0, g)]
    for n in range(SEQ // CH):
        part = slice(n * CH, (n + 1) * CH)
        dk = jnp.dot(dst[part, :], q, preferred_element_type=F32) * SCALE
        dv = jnp.dot(pst[part, :], do, preferred_element_type=F32)
        outs[n][:, cols(1, g)] = dk.astype(BF)
        outs[n][:, cols(2, g)] = dv.astype(BF)


def whole(shape):
    return pl.BlockSpec(shape, lambda g: (0,) * len(shape))


def forward(where, xs):
    return pl.pallas_call(
        forward_kernel,
        grid=(MINE,),
        out_shape=[jax.ShapeDtypeStruct((CH, GRP), BF)] * CHIPS
        + [
            pltpu.HBM((SEQ, GRP), F32),
            pltpu.HBM((MINE, SEQ, SEQ), F32),
            pltpu.HBM((SEQ, 3 * GRP), BF),
        ],
        in_specs=[SMEM] * 3 + [ANY] * CHIPS,
        out_specs=[whole((CH, GRP))] * CHIPS
        + [
            whole((SEQ, GRP)),
            pl.BlockSpec((1, SEQ, SEQ), lambda g: (g, 0, 0)),
            pl.BlockSpec(memory_space=pltpu.HBM),
        ],
        scratch_shapes=[
            pltpu.VMEM((SEQ, 3 * GRP), BF),
            pltpu.SemaphoreType.DMA((CHIPS,)),
            pltpu.SemaphoreType.DMA,
        ],
        compiler_params=pltpu.CompilerParams(vmem_limit_bytes=60 << 20),
        cost_estimate=pl.CostEstimate(
            flops=MINE * 2 * 5 * SEQ * SEQ * DH, bytes_accessed=12 << 20, transcendentals=MINE * SEQ * SEQ
        ),
        name="attend",
    )(*where, *xs)


def backward(where, cs, kept, wide, prob):
    return pl.pallas_call(
        backward_kernel,
        grid=(MINE,),
        out_shape=[jax.ShapeDtypeStruct((CH, 3 * GRP), BF)] * CHIPS,
        in_specs=[SMEM] * 3
        + [ANY] * CHIPS
        + [
            pl.BlockSpec(memory_space=pltpu.HBM),
            whole((SEQ, GRP)),
            pl.BlockSpec((1, SEQ, SEQ), lambda g: (g, 0, 0)),
        ],
        out_specs=[whole((CH, 3 * GRP))] * CHIPS,
        scratch_shapes=[
            pltpu.VMEM((SEQ, 3 * GRP), BF),
            pltpu.VMEM((SEQ, GRP), BF),
            pltpu.VMEM((SEQ, SEQ), BF),
            pltpu.VMEM((SEQ, SEQ), BF),
            pltpu.SemaphoreType.DMA((CHIPS,)),
            pltpu.SemaphoreType.DMA,
        ],
        compiler_params=pltpu.CompilerParams(vmem_limit_bytes=60 << 20),
        cost_estimate=pl.CostEstimate(
            flops=MINE * 2 * 8 * SEQ * SEQ * DH, bytes_accessed=16 << 20, transcendentals=0
        ),
        name="attend_grad",
    )(*where, *cs, kept, wide, prob)


def turn(blocks, sign):
    out = [blocks[0]]
    for k in range(1, CHIPS):
        pairs = [(s, (s + sign * 2 * k) % SHARDS) for s in range(SHARDS)]
        out.append(lax.ppermute(blocks[k], "seq", pairs))
    return out


def swap(block):
    return lax.ppermute(block, "seq", [(s, s ^ 1) for s in range(SHARDS)])


def spread(pieces):
    return lax.all_to_all(pieces, "dp", split_axis=0, concat_axis=0, tiled=True)


def on_device(projected, cotangent, lengths, text_lengths, destinations):
    me = lax.axis_index("seq").astype(jnp.int32)
    at = jnp.stack([me, lax.axis_index("dp").astype(jnp.int32)])
    where = (at, lengths, text_lengths)

    own, other = split_projected(at, projected[0])
    xs = turn(pair(own, swap(other)), 1)
    there = spread(to_pieces(cotangent[0], other))
    here = spread(reorder(destinations, there, False))

    *outs, wide, prob, kept = forward(where, xs)
    os = turn(outs, -1)
    own, other = split_cotangent(at, here, outs[0])
    cs = pair(own, swap(other))
    halfway = spread(join_pieces(at, os, swap(for_sibling(os)), cs[0]))
    cs = turn(cs, 1)

    gs = turn(backward(where, cs, kept, wide, prob), -1)
    home = spread(reorder(destinations, halfway, True, gs[0]))
    projected_grad = join_gradient(at, gs, swap(for_sibling(gs)))
    attended = from_pieces(home)
    return attended[None], projected_grad[None]


def solution(mesh):
    in_specs = (P("dp", "seq", None), P("dp", "seq", None), P(), P(), P())
    out_specs = (P("dp", "seq", None), P("dp", "seq", None))
    return jax.shard_map(
        on_device, mesh=mesh, in_specs=in_specs, out_specs=out_specs, check_vma=False
    )
```

```python
import functools
import jax
import jax.numpy as jnp
from jax import lax
from jax.experimental import pallas as pl
from jax.experimental.pallas import tpu as pltpu
from jax.sharding import PartitionSpec as P

HEADS = 24
DH = 128
CAP = 512
SEQ = 1024
RANKS = 32
SHARDS = 8
ROWS = SEQ // SHARDS
MINE = HEADS // SHARDS
GRP = MINE * DH
WIDTH = HEADS * DH
CHIPS = SHARDS // 2
CH = 2 * ROWS
SCALE = DH ** -0.5
LOGIT = SCALE * 1.4426950408889634
FWD_VMEM = 24
BWD_VMEM = 60
NT = (((1,), (1,)), ((), ()))

ANY = pl.BlockSpec(memory_space=pl.ANY)
SMEM = pl.BlockSpec(memory_space=pltpu.SMEM)
VMEM = pl.BlockSpec(memory_space=pltpu.VMEM)
BF = jnp.bfloat16
F32 = jnp.float32
TOKEN = jax.ShapeDtypeStruct((8, 128), F32)


def copies(body, count, given, late, cost=4):
    def kernel(*refs):
        sems = refs[-1]
        started = []
        used = refs[:given] + refs[given + late : -1]
        for n, (src, dst) in enumerate(body(*used)):
            cp = pltpu.make_async_copy(src, dst, sems.at[n])
            cp.start()
            started.append(cp)
        for cp in started:
            cp.wait()

    return functools.partial(
        pl.pallas_call,
        kernel,
        scratch_shapes=[pltpu.SemaphoreType.DMA((count,))],
        compiler_params=pltpu.CompilerParams(vmem_limit_bytes=1 << 20),
        cost_estimate=pl.CostEstimate(flops=0, bytes_accessed=cost << 20, transcendentals=0),
    )


def place(at, k):
    return lax.bitwise_and(lax.shift_right_logical(at[0], 1) + k, CHIPS - 1), at[0] & 1


def split_projected(at, projected, *late):
    def body(at_ref, x_ref, own, other):
        for k in range(CHIPS):
            chip, core = place(at_ref, k)
            for out, head in ((own, 2 * chip + core), (other, 2 * chip + 1 - core)):
                for t in range(3):
                    start = pl.multiple_of(t * WIDTH + head * GRP, GRP)
                    yield x_ref.at[:, pl.ds(start, GRP)], out.at[k, :, pl.ds(t * GRP, GRP)]

    return copies(body, 6 * CHIPS, 2, len(late))(
        out_shape=[jax.ShapeDtypeStruct((CHIPS, ROWS, 3 * GRP), BF)] * 2,
        in_specs=[SMEM, ANY] + [ANY] * len(late),
        out_specs=[ANY] * 2,
        name="split_projected",
    )(at, projected, *late)


def join_gradient(at, blocks, sibling, *late):
    def body(at_ref, *refs):
        out = refs[-1]
        for k in range(CHIPS):
            chip, core = place(at_ref, k)
            mine = refs[k].at[pl.ds(0, ROWS)], 2 * chip + core
            for src, head in (mine, (refs[CHIPS].at[k], 2 * chip + 1 - core)):
                for t in range(3):
                    start = pl.multiple_of(t * WIDTH + head * GRP, GRP)
                    yield src.at[:, pl.ds(t * GRP, GRP)], out.at[:, pl.ds(start, GRP)]

    return copies(body, 6 * CHIPS, 2 + CHIPS, len(late))(
        out_shape=jax.ShapeDtypeStruct((ROWS, 3 * WIDTH), BF),
        in_specs=[SMEM] + [ANY] * (1 + CHIPS + len(late)),
        out_specs=ANY,
        name="join_gradient",
    )(at, *blocks, sibling, *late)


def pair(own, recv, *late):
    width = own.shape[2]

    def body(own_ref, recv_ref, *outs):
        outs[CHIPS][...] = jnp.zeros_like(outs[CHIPS])
        for k in range(CHIPS):
            yield own_ref.at[k], outs[k].at[pl.ds(0, ROWS)]
            yield recv_ref.at[k], outs[k].at[pl.ds(ROWS, ROWS)]

    return copies(body, 2 * CHIPS, 2, len(late))(
        out_shape=[pltpu.HBM((2 * ROWS, width), BF) if width > GRP else jax.ShapeDtypeStruct((2 * ROWS, width), BF)] * CHIPS
        + [TOKEN],
        in_specs=[ANY] * (2 + len(late)),
        out_specs=[ANY] * CHIPS + [VMEM],
        name="pair",
    )(own, recv, *late)


def for_sibling(blocks, *late):
    width = blocks[0].shape[1]

    def body(*refs):
        for k in range(CHIPS):
            yield refs[k].at[pl.ds(ROWS, ROWS)], refs[CHIPS].at[k]

    return copies(body, CHIPS, CHIPS, len(late))(
        out_shape=jax.ShapeDtypeStruct((CHIPS, ROWS, width), BF),
        in_specs=[ANY] * (CHIPS + len(late)),
        out_specs=ANY,
        name="for_sibling",
    )(*blocks, *late)


def to_pieces(rows, *late):
    def body(x_ref, out):
        for a in range(8):
            for b in range(4):
                yield x_ref.at[pl.ds(16 * a, 16), pl.ds(768 * b, 768)], out.at[4 * a + b]

    return copies(body, RANKS, 1, len(late))(
        out_shape=jax.ShapeDtypeStruct((RANKS, 16, 768), BF),
        in_specs=[ANY] + [ANY] * len(late),
        out_specs=ANY,
        name="to_pieces",
    )(rows, *late)


def from_pieces(pieces, *late):
    def body(x_ref, out):
        for a in range(8):
            for b in range(4):
                yield x_ref.at[4 * a + b], out.at[pl.ds(16 * a, 16), pl.ds(768 * b, 768)]

    return copies(body, RANKS, 1, len(late))(
        out_shape=jax.ShapeDtypeStruct((ROWS, WIDTH), BF),
        in_specs=[ANY] + [ANY] * len(late),
        out_specs=ANY,
        name="from_pieces",
    )(pieces, *late)


def reorder(destinations, pieces, back, *late):
    def body(d_ref, x_ref, out):
        for c in range(RANKS):
            if back:
                yield x_ref.at[c], out.at[d_ref[c]]
            else:
                yield x_ref.at[d_ref[c]], out.at[c]

    return copies(body, RANKS, 2, len(late), 100)(
        out_shape=jax.ShapeDtypeStruct((RANKS, 16, 768), BF),
        in_specs=[SMEM, ANY] + [ANY] * len(late),
        out_specs=ANY,
        name="reorder",
    )(destinations, pieces, *late)


def split_cotangent(at, pieces, *late):
    def body(at_ref, x_ref, own, other):
        for k in range(CHIPS):
            chip, core = place(at_ref, k)
            for out, half in ((own, core), (other, 1 - core)):
                start = pl.multiple_of(half * GRP, GRP)
                for a in range(8):
                    src = x_ref.at[4 * a + chip, :, pl.ds(start, GRP)]
                    yield src, out.at[k, pl.ds(16 * a, 16)]

    return copies(body, 16 * CHIPS, 2, len(late))(
        out_shape=[jax.ShapeDtypeStruct((CHIPS, ROWS, GRP), BF)] * 2,
        in_specs=[SMEM, ANY] + [ANY] * len(late),
        out_specs=[ANY] * 2,
        name="split_cotangent",
    )(at, pieces, *late)


def join_pieces(at, blocks, sibling, *late):
    def body(at_ref, *refs):
        out = refs[-1]
        for k in range(CHIPS):
            chip, core = place(at_ref, k)
            for src, half in ((refs[k], core), (refs[CHIPS].at[k], 1 - core)):
                start = pl.multiple_of(half * GRP, GRP)
                for a in range(8):
                    yield src.at[pl.ds(16 * a, 16)], out.at[4 * a + chip, :, pl.ds(start, GRP)]

    return copies(body, 16 * CHIPS, 2 + CHIPS, len(late))(
        out_shape=jax.ShapeDtypeStruct((RANKS, 16, 768), BF),
        in_specs=[SMEM] + [ANY] * (1 + CHIPS + len(late)),
        out_specs=ANY,
        name="join_pieces",
    )(at, *blocks, sibling, *late)


def live_rows(at, lengths, text_lengths):
    row = lax.broadcasted_iota(jnp.int32, (SEQ, DH), 0)
    chip = lax.bitwise_and((at[0] >> 1) + CHIPS - lax.shift_right_logical(row, 8), CHIPS - 1)
    core = lax.bitwise_xor(at[0] & 1, lax.bitwise_and(lax.shift_right_logical(row, 7), 1))
    pos = (2 * chip + core) * ROWS + lax.bitwise_and(row, ROWS - 1)
    latent, text = lengths[at[1]], text_lengths[at[1]]
    return (pos < latent) | ((pos >= CAP) & (pos < CAP + text))


def cols(part, head):
    return pl.ds(pl.multiple_of(part * GRP + head * DH, DH), DH)


def moves(refs, held, sems, inward):
    out = []
    for k in range(CHIPS):
        rows = held.at[pl.ds(k * CH, CH)]
        src, dst = (refs[k], rows) if inward else (rows, refs[k])
        out.append(pltpu.make_async_copy(src, dst, sems.at[k]))
    return out


def run(started):
    for cp in started:
        cp.start()
    for cp in started:
        cp.wait()


def thirds(value):
    hi = value.astype(BF).astype(F32)
    mid = (value - hi).astype(BF).astype(F32)
    return hi, mid, value - hi - mid


def forward_kernel(at, lengths, text_lengths, *refs):
    xs = refs[:CHIPS]
    outs = refs[CHIPS : 2 * CHIPS]
    wide, norm, held, done, in_sems, out_sems = refs[2 * CHIPS :]
    g = pl.program_id(0)

    @pl.when(g == 0)
    def _():
        run(moves(xs, held, in_sems, True))

    live = live_rows(at, lengths, text_lengths)
    lane = lax.broadcasted_iota(jnp.int32, (SEQ, DH), 1)
    dead = jnp.where(live | (lane > 0), 0.0, -1e30).astype(BF)
    unit = jnp.where(lane == 0, 1.0, 0.0).astype(BF)
    q = jnp.concatenate([held[:, cols(0, g)], unit], axis=1)
    k = jnp.concatenate([held[:, cols(1, g)], dead], axis=1)
    vt = held[:, cols(2, g)].T
    livef = live.astype(F32)
    ahead = lax.dot_general(k, q[0:CH], NT, preferred_element_type=F32)
    for n in range(SEQ // CH):
        part = slice(n * CH, (n + 1) * CH)
        s = ahead
        if n + 1 < SEQ // CH:
            ahead = lax.dot_general(
                k, q[(n + 1) * CH : (n + 2) * CH], NT, preferred_element_type=F32
            )
        top = jnp.max(s, axis=0, keepdims=True)
        e = jnp.exp2((s - top) * LOGIT)
        total = jnp.sum(e, axis=0, keepdims=True)
        norm[0, :, part] = top + jnp.log2(total) * (1.0 / LOGIT)
        p = e.astype(BF)
        rest = (e - p.astype(F32)).astype(BF)
        o = jnp.dot(vt, p, preferred_element_type=F32)
        o = o + jnp.dot(vt, rest, preferred_element_type=F32)
        o = (o * (1.0 / total)).T
        wide[0, part, :] = o
        done[part, cols(0, g)] = (o * livef[part]).astype(BF)

    @pl.when(g == MINE - 1)
    def _():
        run(moves(outs, done, out_sems, False))


def backward_kernel(at, lengths, text_lengths, *refs):
    xs = refs[:CHIPS]
    cs = refs[CHIPS : 2 * CHIPS]
    wide, norm = refs[2 * CHIPS : 2 * CHIPS + 2]
    outs = refs[2 * CHIPS + 2 : 3 * CHIPS + 2]
    token, held, cot, done, dst, pst, in_sems, cot_sems, out_sems = refs[3 * CHIPS + 2 :]
    g = pl.program_id(0)

    @pl.when(g == 0)
    def _():
        run(moves(xs, held, in_sems, True) + moves(cs, cot, cot_sems, True))
        token[...] = jnp.zeros_like(token)

    live = live_rows(at, lengths, text_lengths)
    lane = lax.broadcasted_iota(jnp.int32, (SEQ, DH), 1)
    do = jnp.where(live, cot[:, cols(0, g)], jnp.zeros((), BF))
    dot = jnp.sum(do.astype(F32) * wide[0], axis=1, keepdims=True)
    hi, mid, low = thirds(dot)
    less = jnp.where(lane == 0, -hi, jnp.where(lane == 1, -mid, jnp.where(lane == 2, -low, 0.0)))
    dox = jnp.concatenate([do, less.astype(BF)], axis=1)
    units = jnp.where(lane < 3, 1.0, 0.0).astype(BF)
    vx = jnp.concatenate([held[:, cols(2, g)], units], axis=1)
    hi, mid, low = thirds(norm[0].T)
    less = jnp.where(lane == 0, -hi, jnp.where(lane == 1, -mid, jnp.where(lane == 2, -low, 0.0)))
    less = jnp.where(lane == 3, 1.0, less).astype(BF)
    dead = jnp.where(lane < 3, 1.0, jnp.where(live | (lane > 3), 0.0, -1e30)).astype(BF)
    qx = jnp.concatenate([held[:, cols(0, g)], less], axis=1)
    kx = jnp.concatenate([held[:, cols(1, g)], dead], axis=1)
    kt = held[:, cols(1, g)].T
    for n in range(SEQ // CH):
        part = slice(n * CH, (n + 1) * CH)
        s = lax.dot_general(kx, qx[part], NT, preferred_element_type=F32)
        dp = lax.dot_general(vx, dox[part], NT, preferred_element_type=F32)
        p = jnp.exp2(s * LOGIT)
        pst[:, part] = p.astype(BF)
        ds = (p * dp).astype(BF)
        dst[:, part] = ds
        dq = jnp.dot(kt, ds, preferred_element_type=F32).T * SCALE
        done[part, cols(0, g)] = dq.astype(BF)
    q = held[:, cols(0, g)]
    for n in range(SEQ // CH):
        part = slice(n * CH, (n + 1) * CH)
        dk = jnp.dot(dst[part, :], q, preferred_element_type=F32) * SCALE
        dv = jnp.dot(pst[part, :], do, preferred_element_type=F32)
        done[part, cols(1, g)] = dk.astype(BF)
        done[part, cols(2, g)] = dv.astype(BF)

    @pl.when(g == MINE - 1)
    def _():
        run(moves(outs, done, out_sems, False))


WIDE = pl.BlockSpec((1, SEQ, DH), lambda g: (g, 0, 0))
NORM = pl.BlockSpec((1, 1, SEQ), lambda g: (g, 0, 0))


def forward(where, xs):
    return pl.pallas_call(
        forward_kernel,
        grid=(MINE,),
        out_shape=[jax.ShapeDtypeStruct((CH, GRP), BF)] * CHIPS
        + [pltpu.HBM((MINE, SEQ, DH), F32), pltpu.HBM((MINE, 1, SEQ), F32)],
        in_specs=[SMEM] * 3 + [ANY] * CHIPS,
        out_specs=[ANY] * CHIPS + [WIDE, NORM],
        scratch_shapes=[
            pltpu.VMEM((SEQ, 3 * GRP), BF),
            pltpu.VMEM((SEQ, GRP), BF),
            pltpu.SemaphoreType.DMA((CHIPS,)),
            pltpu.SemaphoreType.DMA((CHIPS,)),
        ],
        compiler_params=pltpu.CompilerParams(vmem_limit_bytes=FWD_VMEM << 20),
        cost_estimate=pl.CostEstimate(
            flops=20 * MINE * 2 * 5 * SEQ * SEQ * DH, bytes_accessed=12 << 20, transcendentals=MINE * SEQ * SEQ
        ),
        name="attend",
    )(*where, *xs)


def backward(where, cs, xs, wide, norm):
    return pl.pallas_call(
        backward_kernel,
        grid=(MINE,),
        out_shape=[jax.ShapeDtypeStruct((CH, 3 * GRP), BF)] * CHIPS + [TOKEN],
        in_specs=[SMEM] * 3 + [ANY] * (2 * CHIPS) + [WIDE, NORM],
        out_specs=[ANY] * CHIPS + [pl.BlockSpec((8, 128), lambda g: (0, 0))],
        scratch_shapes=[
            pltpu.VMEM((SEQ, 3 * GRP), BF),
            pltpu.VMEM((SEQ, GRP), BF),
            pltpu.VMEM((SEQ, 3 * GRP), BF),
            pltpu.VMEM((SEQ, SEQ), BF),
            pltpu.VMEM((SEQ, SEQ), BF),
            pltpu.SemaphoreType.DMA((CHIPS,)),
            pltpu.SemaphoreType.DMA((CHIPS,)),
            pltpu.SemaphoreType.DMA((CHIPS,)),
        ],
        compiler_params=pltpu.CompilerParams(vmem_limit_bytes=BWD_VMEM << 20),
        cost_estimate=pl.CostEstimate(
            flops=20 * MINE * 2 * 8 * SEQ * SEQ * DH, bytes_accessed=16 << 20, transcendentals=0
        ),
        name="attend_grad",
    )(*where, *xs, *cs, wide, norm)


def turn(blocks, sign):
    out = [blocks[0]]
    for k in range(1, CHIPS):
        pairs = [(s, (s + sign * 2 * k) % SHARDS) for s in range(SHARDS)]
        out.append(lax.ppermute(blocks[k], "seq", pairs))
    return out


def swap(block):
    return lax.ppermute(block, "seq", [(s, s ^ 1) for s in range(SHARDS)])


def spread(pieces):
    return lax.all_to_all(pieces, "dp", split_axis=0, concat_axis=0, tiled=True)


def on_device(projected, cotangent, lengths, text_lengths, destinations):
    me = lax.axis_index("seq").astype(jnp.int32)
    at = jnp.stack([me, lax.axis_index("dp").astype(jnp.int32)])
    where = (at, lengths, text_lengths)

    own, other = split_projected(at, projected[0])
    *xs, paired = pair(own, swap(other))
    xs = turn(xs, 1)
    there = spread(to_pieces(cotangent[0]))
    here = spread(reorder(destinations, there, False, paired))

    *outs, wide, norm = forward(where, xs)
    os = turn(outs, -1)
    own, other = split_cotangent(at, here, norm)
    *cs, paired = pair(own, swap(other))
    halfway = spread(join_pieces(at, os, swap(for_sibling(os)), paired))
    cs = turn(cs, 1)

    *gs, graded = backward(where, cs, xs, wide, norm)
    gs = turn(gs, -1)
    home = spread(reorder(destinations, halfway, True, graded))
    projected_grad = join_gradient(at, gs, swap(for_sibling(gs)))
    attended = from_pieces(home)
    return attended[None], projected_grad[None]


def solution(mesh):
    in_specs = (P("dp", "seq", None), P("dp", "seq", None), P(), P(), P())
    out_specs = (P("dp", "seq", None), P("dp", "seq", None))
    return jax.shard_map(
        on_device, mesh=mesh, in_specs=in_specs, out_specs=out_specs, check_vma=False
    )
```

```python
import functools
import jax
import jax.numpy as jnp
from jax import lax
from jax.experimental import pallas as pl
from jax.experimental.pallas import tpu as pltpu
from jax.sharding import PartitionSpec as P

HEADS = 24
DH = 128
CAP = 512
SEQ = 1024
RANKS = 32
SHARDS = 8
ROWS = SEQ // SHARDS
MINE = HEADS // SHARDS
GRP = MINE * DH
WIDTH = HEADS * DH
CHIPS = SHARDS // 2
IC = 512
CH = 2 * ROWS
SCALE = DH ** -0.5
LOGIT = SCALE * 1.4426950408889634
FWD_VMEM = 24
BWD_VMEM = 32
NT = (((1,), (1,)), ((), ()))

ANY = pl.BlockSpec(memory_space=pl.ANY)
SMEM = pl.BlockSpec(memory_space=pltpu.SMEM)
VMEM = pl.BlockSpec(memory_space=pltpu.VMEM)
BF = jnp.bfloat16
F32 = jnp.float32
TOKEN = jax.ShapeDtypeStruct((8, 128), F32)


def copies(body, count, given, late, cost=4):
    def kernel(*refs):
        sems = refs[-1]
        started = []
        used = refs[:given] + refs[given + late : -1]
        for n, (src, dst) in enumerate(body(*used)):
            cp = pltpu.make_async_copy(src, dst, sems.at[n])
            cp.start()
            started.append(cp)
        for cp in started:
            cp.wait()

    return functools.partial(
        pl.pallas_call,
        kernel,
        scratch_shapes=[pltpu.SemaphoreType.DMA((count,))],
        compiler_params=pltpu.CompilerParams(vmem_limit_bytes=1 << 20),
        cost_estimate=pl.CostEstimate(flops=0, bytes_accessed=cost << 20, transcendentals=0),
    )


def place(at, k):
    return lax.bitwise_and(lax.shift_right_logical(at[0], 1) + k, CHIPS - 1), at[0] & 1


def split_projected(at, projected, *late):
    def body(at_ref, x_ref, own, other):
        for k in range(CHIPS):
            chip, core = place(at_ref, k)
            for out, head in ((own, 2 * chip + core), (other, 2 * chip + 1 - core)):
                for t in range(3):
                    start = pl.multiple_of(t * WIDTH + head * GRP, GRP)
                    yield x_ref.at[:, pl.ds(start, GRP)], out.at[k, :, pl.ds(t * GRP, GRP)]

    return copies(body, 6 * CHIPS, 2, len(late))(
        out_shape=[jax.ShapeDtypeStruct((CHIPS, ROWS, 3 * GRP), BF)] * 2,
        in_specs=[SMEM, ANY] + [ANY] * len(late),
        out_specs=[ANY] * 2,
        name="split_projected",
    )(at, projected, *late)


def join_gradient(at, blocks, sibling, *late):
    def body(at_ref, *refs):
        out = refs[-1]
        for k in range(CHIPS):
            chip, core = place(at_ref, k)
            mine = refs[k].at[pl.ds(0, ROWS)], 2 * chip + core
            for src, head in (mine, (refs[CHIPS].at[k], 2 * chip + 1 - core)):
                for t in range(3):
                    start = pl.multiple_of(t * WIDTH + head * GRP, GRP)
                    yield src.at[:, pl.ds(t * GRP, GRP)], out.at[:, pl.ds(start, GRP)]

    return copies(body, 6 * CHIPS, 2 + CHIPS, len(late))(
        out_shape=jax.ShapeDtypeStruct((ROWS, 3 * WIDTH), BF),
        in_specs=[SMEM] + [ANY] * (1 + CHIPS + len(late)),
        out_specs=ANY,
        name="join_gradient",
    )(at, *blocks, sibling, *late)


def pair(own, recv, *late):
    width = own.shape[2]

    def body(own_ref, recv_ref, *outs):
        outs[CHIPS][...] = jnp.zeros_like(outs[CHIPS])
        for k in range(CHIPS):
            yield own_ref.at[k], outs[k].at[pl.ds(0, ROWS)]
            yield recv_ref.at[k], outs[k].at[pl.ds(ROWS, ROWS)]

    return copies(body, 2 * CHIPS, 2, len(late))(
        out_shape=[pltpu.HBM((2 * ROWS, width), BF)] * CHIPS
        + [TOKEN],
        in_specs=[ANY] * (2 + len(late)),
        out_specs=[ANY] * CHIPS + [VMEM],
        name="pair",
    )(own, recv, *late)


def for_sibling(blocks, *late):
    width = blocks[0].shape[1]

    def body(*refs):
        for k in range(CHIPS):
            yield refs[k].at[pl.ds(ROWS, ROWS)], refs[CHIPS].at[k]

    return copies(body, CHIPS, CHIPS, len(late))(
        out_shape=jax.ShapeDtypeStruct((CHIPS, ROWS, width), BF),
        in_specs=[ANY] * (CHIPS + len(late)),
        out_specs=ANY,
        name="for_sibling",
    )(*blocks, *late)


def to_pieces(rows, *late):
    def body(x_ref, out):
        for a in range(8):
            for b in range(4):
                yield x_ref.at[pl.ds(16 * a, 16), pl.ds(768 * b, 768)], out.at[4 * a + b]

    return copies(body, RANKS, 1, len(late))(
        out_shape=jax.ShapeDtypeStruct((RANKS, 16, 768), BF),
        in_specs=[ANY] + [ANY] * len(late),
        out_specs=ANY,
        name="to_pieces",
    )(rows, *late)


def from_pieces(pieces, *late):
    def body(x_ref, out):
        for a in range(8):
            for b in range(4):
                yield x_ref.at[4 * a + b], out.at[pl.ds(16 * a, 16), pl.ds(768 * b, 768)]

    return copies(body, RANKS, 1, len(late))(
        out_shape=jax.ShapeDtypeStruct((ROWS, WIDTH), BF),
        in_specs=[ANY] + [ANY] * len(late),
        out_specs=ANY,
        name="from_pieces",
    )(pieces, *late)


def reorder(destinations, pieces, back, *late):
    def body(d_ref, x_ref, out):
        for c in range(RANKS):
            if back:
                yield x_ref.at[c], out.at[d_ref[c]]
            else:
                yield x_ref.at[d_ref[c]], out.at[c]

    return copies(body, RANKS, 2, len(late), 100)(
        out_shape=jax.ShapeDtypeStruct((RANKS, 16, 768), BF),
        in_specs=[SMEM, ANY] + [ANY] * len(late),
        out_specs=ANY,
        name="reorder",
    )(destinations, pieces, *late)


def split_cotangent(at, pieces, *late):
    def body(at_ref, x_ref, own, other):
        for k in range(CHIPS):
            chip, core = place(at_ref, k)
            for out, half in ((own, core), (other, 1 - core)):
                start = pl.multiple_of(half * GRP, GRP)
                for a in range(8):
                    src = x_ref.at[4 * a + chip, :, pl.ds(start, GRP)]
                    yield src, out.at[k, pl.ds(16 * a, 16)]

    return copies(body, 16 * CHIPS, 2, len(late))(
        out_shape=[jax.ShapeDtypeStruct((CHIPS, ROWS, GRP), BF)] * 2,
        in_specs=[SMEM, ANY] + [ANY] * len(late),
        out_specs=[ANY] * 2,
        name="split_cotangent",
    )(at, pieces, *late)


def join_pieces(at, blocks, sibling, *late):
    def body(at_ref, *refs):
        out = refs[-1]
        for k in range(CHIPS):
            chip, core = place(at_ref, k)
            for src, half in ((refs[k], core), (refs[CHIPS].at[k], 1 - core)):
                start = pl.multiple_of(half * GRP, GRP)
                for a in range(8):
                    yield src.at[pl.ds(16 * a, 16)], out.at[4 * a + chip, :, pl.ds(start, GRP)]

    return copies(body, 16 * CHIPS, 2 + CHIPS, len(late))(
        out_shape=jax.ShapeDtypeStruct((RANKS, 16, 768), BF),
        in_specs=[SMEM] + [ANY] * (1 + CHIPS + len(late)),
        out_specs=ANY,
        name="join_pieces",
    )(at, *blocks, sibling, *late)


def live_rows(at, lengths, text_lengths):
    row = lax.broadcasted_iota(jnp.int32, (SEQ, DH), 0)
    chip = lax.bitwise_and((at[0] >> 1) + CHIPS - lax.shift_right_logical(row, 8), CHIPS - 1)
    core = lax.bitwise_xor(at[0] & 1, lax.bitwise_and(lax.shift_right_logical(row, 7), 1))
    pos = (2 * chip + core) * ROWS + lax.bitwise_and(row, ROWS - 1)
    latent, text = lengths[at[1]], text_lengths[at[1]]
    return (pos < latent) | ((pos >= CAP) & (pos < CAP + text))


def cols(part, head):
    return pl.ds(part * GRP + head * DH, DH)


def moves(refs, held, sems, parts, inward):
    heads = []
    for g in range(MINE):
        out = []
        for k in range(CHIPS):
            for t in range(parts):
                block = refs[k].at[:, cols(t, g)]
                rows = held.at[pl.ds(k * CH, CH), cols(t, g)]
                src, dst = (block, rows) if inward else (rows, block)
                out.append(pltpu.make_async_copy(src, dst, sems.at[g, k, t]))
        heads.append(out)
    return heads


def begin(started):
    for cp in started:
        cp.start()


def finish(started):
    for cp in started:
        cp.wait()


def thirds(value):
    hi = value.astype(BF).astype(F32)
    mid = (value - hi).astype(BF).astype(F32)
    return hi, mid, value - hi - mid


def forward_kernel(at, lengths, text_lengths, *refs):
    xs = refs[:CHIPS]
    outs = refs[CHIPS : 2 * CHIPS]
    wide, norm, token, held, done, wide_held, in_sems, out_sems, wide_sems = refs[2 * CHIPS :]
    token[...] = jnp.zeros_like(token)

    arriving = moves(xs, held, in_sems, 3, True)
    leaving = moves(outs, done, out_sems, 1, False)
    for g in range(MINE):
        leaving[g].append(pltpu.make_async_copy(wide_held.at[g], wide.at[g], wide_sems.at[g]))
        begin(arriving[g])

    live = live_rows(at, lengths, text_lengths)
    for g in range(MINE):
        finish(arriving[g])
        lane = lax.broadcasted_iota(jnp.int32, (SEQ, DH), 1)
        dead = jnp.where(live | (lane > 0), 0.0, -1e30).astype(BF)
        unit = jnp.where(lane == 0, 1.0, 0.0).astype(BF)
        q = jnp.concatenate([held[:, cols(0, g)], unit], axis=1)
        k = jnp.concatenate([held[:, cols(1, g)], dead], axis=1)
        vt = held[:, cols(2, g)].T
        livef = live.astype(F32)
        ahead = lax.dot_general(k, q[0:CH], NT, preferred_element_type=F32)
        for n in range(SEQ // CH):
            part = slice(n * CH, (n + 1) * CH)
            s = ahead
            if n + 1 < SEQ // CH:
                ahead = lax.dot_general(
                    k, q[(n + 1) * CH : (n + 2) * CH], NT, preferred_element_type=F32
                )
            top = jnp.max(s, axis=0, keepdims=True)
            e = jnp.exp2((s - top) * LOGIT)
            total = jnp.sum(e, axis=0, keepdims=True)
            norm[g, :, part] = top + jnp.log2(total) * (1.0 / LOGIT)
            p = e.astype(BF)
            rest = (e - p.astype(F32)).astype(BF)
            o = jnp.dot(vt, p, preferred_element_type=F32)
            o = o + jnp.dot(vt, rest, preferred_element_type=F32)
            o = (o * (1.0 / total)).T
            wide_held[g, part, :] = o
            done[part, cols(0, g)] = (o * livef[part]).astype(BF)

        begin(leaving[g])
    for g in range(MINE):
        finish(leaving[g])


def backward_kernel(at, lengths, text_lengths, *refs):
    xs = refs[:CHIPS]
    cs = refs[CHIPS : 2 * CHIPS]
    wide, norm = refs[2 * CHIPS : 2 * CHIPS + 2]
    outs = refs[2 * CHIPS + 2 : 3 * CHIPS + 2]
    token, held, cot, done, dst, pst, wide_held, in_sems, cot_sems, out_sems, wide_sems = refs[3 * CHIPS + 2 :]

    arriving = moves(xs, held, in_sems, 3, True)
    coming = moves(cs, cot, cot_sems, 1, True)
    leaving = moves(outs, done, out_sems, 3, False)
    for g in range(MINE):
        arriving[g].append(pltpu.make_async_copy(wide.at[g], wide_held.at[g], wide_sems.at[g]))
        begin(arriving[g] + coming[g])
    token[...] = jnp.zeros_like(token)

    live = live_rows(at, lengths, text_lengths)
    for g in range(MINE):
        finish(arriving[g] + coming[g])
        lane = lax.broadcasted_iota(jnp.int32, (SEQ, DH), 1)
        do = jnp.where(live, cot[:, cols(0, g)], jnp.zeros((), BF))
        dot = jnp.sum(do.astype(F32) * wide_held[g], axis=1, keepdims=True)
        hi, mid, low = thirds(dot)
        less = jnp.where(lane == 0, -hi, jnp.where(lane == 1, -mid, jnp.where(lane == 2, -low, 0.0)))
        dox = jnp.concatenate([do, less.astype(BF)], axis=1)
        units = jnp.where(lane < 3, 1.0, 0.0).astype(BF)
        vx = jnp.concatenate([held[:, cols(2, g)], units], axis=1)
        hi, mid, low = thirds(norm[g].T)
        less = jnp.where(lane == 0, -hi, jnp.where(lane == 1, -mid, jnp.where(lane == 2, -low, 0.0)))
        less = jnp.where(lane == 3, 1.0, less).astype(BF)
        dead = jnp.where(lane < 3, 1.0, jnp.where(live | (lane > 3), 0.0, -1e30)).astype(BF)
        qx = jnp.concatenate([held[:, cols(0, g)], less], axis=1)
        kx = jnp.concatenate([held[:, cols(1, g)], dead], axis=1)
        kt = held[:, cols(1, g)].T
        for n in range(SEQ // IC):
            part = slice(n * IC, (n + 1) * IC)
            s = lax.dot_general(kx, qx[part], NT, preferred_element_type=F32)
            dp = lax.dot_general(vx, dox[part], NT, preferred_element_type=F32)
            p = jnp.exp2(s * LOGIT)
            pst[:, part] = p.astype(BF)
            ds = (p * dp).astype(BF)
            dst[:, part] = ds
            dq = jnp.dot(kt, ds, preferred_element_type=F32).T * SCALE
            done[part, cols(0, g)] = dq.astype(BF)
        q = held[:, cols(0, g)]
        for n in range(SEQ // IC):
            part = slice(n * IC, (n + 1) * IC)
            dk = jnp.dot(dst[part, :], q, preferred_element_type=F32) * SCALE
            dv = jnp.dot(pst[part, :], do, preferred_element_type=F32)
            done[part, cols(1, g)] = dk.astype(BF)
            done[part, cols(2, g)] = dv.astype(BF)

        begin(leaving[g])
    for g in range(MINE):
        finish(leaving[g])


NORM = pl.BlockSpec((MINE, 1, SEQ), lambda g: (0, 0, 0))


def forward(where, xs):
    return pl.pallas_call(
        forward_kernel,
        grid=(1,),
        out_shape=[jax.ShapeDtypeStruct((CH, GRP), BF)] * CHIPS
        + [pltpu.HBM((MINE, SEQ, DH), F32), pltpu.HBM((MINE, 1, SEQ), F32), TOKEN],
        in_specs=[SMEM] * 3 + [ANY] * CHIPS,
        out_specs=[ANY] * (CHIPS + 1) + [NORM, pl.BlockSpec((8, 128), lambda g: (0, 0))],
        scratch_shapes=[
            pltpu.VMEM((SEQ, 3 * GRP), BF),
            pltpu.VMEM((SEQ, GRP), BF),
            pltpu.VMEM((MINE, SEQ, DH), F32),
            pltpu.SemaphoreType.DMA((MINE, CHIPS, 3)),
            pltpu.SemaphoreType.DMA((MINE, CHIPS, 1)),
            pltpu.SemaphoreType.DMA((MINE,)),
        ],
        compiler_params=pltpu.CompilerParams(vmem_limit_bytes=FWD_VMEM << 20),
        cost_estimate=pl.CostEstimate(
            flops=20 * MINE * 2 * 5 * SEQ * SEQ * DH, bytes_accessed=12 << 20, transcendentals=MINE * SEQ * SEQ
        ),
        name="attend",
    )(*where, *xs)


def backward(where, cs, xs, wide, norm):
    return pl.pallas_call(
        backward_kernel,
        grid=(1,),
        out_shape=[jax.ShapeDtypeStruct((CH, 3 * GRP), BF)] * CHIPS + [TOKEN],
        in_specs=[SMEM] * 3 + [ANY] * (2 * CHIPS) + [ANY, NORM],
        out_specs=[ANY] * CHIPS + [pl.BlockSpec((8, 128), lambda g: (0, 0))],
        scratch_shapes=[
            pltpu.VMEM((SEQ, 3 * GRP), BF),
            pltpu.VMEM((SEQ, GRP), BF),
            pltpu.VMEM((SEQ, 3 * GRP), BF),
            pltpu.VMEM((SEQ, SEQ), BF),
            pltpu.VMEM((SEQ, SEQ), BF),
            pltpu.VMEM((MINE, SEQ, DH), F32),
            pltpu.SemaphoreType.DMA((MINE, CHIPS, 3)),
            pltpu.SemaphoreType.DMA((MINE, CHIPS, 1)),
            pltpu.SemaphoreType.DMA((MINE, CHIPS, 3)),
            pltpu.SemaphoreType.DMA((MINE,)),
        ],
        compiler_params=pltpu.CompilerParams(vmem_limit_bytes=BWD_VMEM << 20),
        cost_estimate=pl.CostEstimate(
            flops=20 * MINE * 2 * 8 * SEQ * SEQ * DH, bytes_accessed=16 << 20, transcendentals=0
        ),
        name="attend_grad",
    )(*where, *xs, *cs, wide, norm)


def turn(blocks, sign):
    out = [blocks[0]]
    for k in range(1, CHIPS):
        pairs = [(s, (s + sign * 2 * k) % SHARDS) for s in range(SHARDS)]
        out.append(lax.ppermute(blocks[k], "seq", pairs))
    return out


def swap(block):
    return lax.ppermute(block, "seq", [(s, s ^ 1) for s in range(SHARDS)])


def spread(pieces):
    return lax.all_to_all(pieces, "dp", split_axis=0, concat_axis=0, tiled=True)


def on_device(projected, cotangent, lengths, text_lengths, destinations):
    me = lax.axis_index("seq").astype(jnp.int32)
    at = jnp.stack([me, lax.axis_index("dp").astype(jnp.int32)])
    where = (at, lengths, text_lengths)

    own, other = split_projected(at, projected[0])
    *xs, paired = pair(own, swap(other))
    xs = turn(xs, 1)
    there = spread(to_pieces(cotangent[0]))
    here = spread(reorder(destinations, there, False, paired))

    *outs, wide, norm, attended_once = forward(where, xs)
    os = turn(outs, -1)
    own, other = split_cotangent(at, here, attended_once)
    *cs, paired = pair(own, swap(other))
    halfway = spread(join_pieces(at, os, swap(for_sibling(os)), paired))
    cs = turn(cs, 1)

    *gs, graded = backward(where, cs, xs, wide, norm)
    gs = turn(gs, -1)
    home = spread(reorder(destinations, halfway, True, graded))
    projected_grad = join_gradient(at, gs, swap(for_sibling(gs)))
    attended = from_pieces(home)
    return attended[None], projected_grad[None]


def solution(mesh):
    in_specs = (P("dp", "seq", None), P("dp", "seq", None), P(), P(), P())
    out_specs = (P("dp", "seq", None), P("dp", "seq", None))
    return jax.shard_map(
        on_device, mesh=mesh, in_specs=in_specs, out_specs=out_specs, check_vma=False
    )
```

```python
import functools
import jax
import jax.numpy as jnp
from jax import lax
from jax.experimental import pallas as pl
from jax.experimental.pallas import tpu as pltpu
from jax.sharding import PartitionSpec as P

HEADS = 24
DH = 128
CAP = 512
SEQ = 1024
RANKS = 32
SHARDS = 8
ROWS = SEQ // SHARDS
MINE = HEADS // SHARDS
GRP = MINE * DH
WIDTH = HEADS * DH
CHIPS = SHARDS // 2
PIECES = (8, 4, 16, 768)
IC = 512
CH = 2 * ROWS
SCALE = DH ** -0.5
LOGIT = SCALE * 1.4426950408889634
FWD_VMEM = 24
BWD_VMEM = 32
NT = (((1,), (1,)), ((), ()))

ANY = pl.BlockSpec(memory_space=pl.ANY)
SMEM = pl.BlockSpec(memory_space=pltpu.SMEM)
VMEM = pl.BlockSpec(memory_space=pltpu.VMEM)
BF = jnp.bfloat16
F32 = jnp.float32
TOKEN = jax.ShapeDtypeStruct((8, 128), F32)


def copies(body, count, given, late, cost=4):
    def kernel(*refs):
        sems = refs[-1]
        started = []
        used = refs[:given] + refs[given + late : -1]
        for n, (src, dst) in enumerate(body(*used)):
            cp = pltpu.make_async_copy(src, dst, sems.at[n])
            cp.start()
            started.append(cp)
        for cp in started:
            cp.wait()

    return functools.partial(
        pl.pallas_call,
        kernel,
        scratch_shapes=[pltpu.SemaphoreType.DMA((count,))],
        compiler_params=pltpu.CompilerParams(vmem_limit_bytes=1 << 20),
        cost_estimate=pl.CostEstimate(flops=0, bytes_accessed=cost << 20, transcendentals=0),
    )


def place(at, k):
    return lax.bitwise_and(lax.shift_right_logical(at[0], 1) + k, CHIPS - 1), at[0] & 1


def split_projected(at, projected, *late):
    def body(at_ref, x_ref, own, other):
        for k in range(CHIPS):
            chip, core = place(at_ref, k)
            for out, head in ((own, 2 * chip + core), (other, 2 * chip + 1 - core)):
                for t in range(3):
                    start = pl.multiple_of(t * WIDTH + head * GRP, GRP)
                    yield x_ref.at[:, pl.ds(start, GRP)], out.at[k, :, pl.ds(t * GRP, GRP)]

    return copies(body, 6 * CHIPS, 2, len(late))(
        out_shape=[jax.ShapeDtypeStruct((CHIPS, ROWS, 3 * GRP), BF)] * 2,
        in_specs=[SMEM, ANY] + [ANY] * len(late),
        out_specs=[ANY] * 2,
        name="split_projected",
    )(at, projected, *late)


def join_gradient(at, parts, own, so_far, *late):
    def body(at_ref, *refs):
        out = refs[-1]
        for k in range(CHIPS):
            chip, core = place(at_ref, k)
            src = refs[k].at[pl.ds(0, ROWS)] if own else refs[0].at[k]
            head = 2 * chip + (core if own else 1 - core)
            for t in range(3):
                start = pl.multiple_of(t * WIDTH + head * GRP, GRP)
                yield src.at[:, pl.ds(t * GRP, GRP)], out.at[:, pl.ds(start, GRP)]

    given = (at, *parts, *so_far)
    return copies(body, 3 * CHIPS, len(given), len(late))(
        out_shape=pltpu.HBM((ROWS, 3 * WIDTH), BF),
        in_specs=[SMEM] + [ANY] * (len(given) - 1 + len(late)),
        out_specs=ANY,
        input_output_aliases={} if own else {2: 0},
        name="join_gradient",
    )(*given, *late)


def pair(own, recv, *late):
    width = own.shape[2]

    def body(own_ref, recv_ref, *outs):
        outs[CHIPS][...] = jnp.zeros_like(outs[CHIPS])
        for k in range(CHIPS):
            yield own_ref.at[k], outs[k].at[pl.ds(0, ROWS)]
            yield recv_ref.at[k], outs[k].at[pl.ds(ROWS, ROWS)]

    return copies(body, 2 * CHIPS, 2, len(late))(
        out_shape=[pltpu.HBM((2 * ROWS, width), BF)] * CHIPS
        + [TOKEN],
        in_specs=[ANY] * (2 + len(late)),
        out_specs=[ANY] * CHIPS + [VMEM],
        name="pair",
    )(own, recv, *late)


def for_sibling(blocks, *late):
    width = blocks[0].shape[1]

    def body(*refs):
        for k in range(CHIPS):
            yield refs[k].at[pl.ds(ROWS, ROWS)], refs[CHIPS].at[k]

    return copies(body, CHIPS, CHIPS, len(late))(
        out_shape=jax.ShapeDtypeStruct((CHIPS, ROWS, width), BF),
        in_specs=[ANY] * (CHIPS + len(late)),
        out_specs=ANY,
        name="for_sibling",
    )(*blocks, *late)


def to_pieces(rows, *late):
    def body(x_ref, out):
        for b in range(4):
            yield x_ref.at[:, :, pl.ds(768 * b, 768)], out.at[:, b]

    pieces = copies(body, 4, 1, len(late))(
        out_shape=jax.ShapeDtypeStruct(PIECES, BF),
        in_specs=[ANY] + [ANY] * len(late),
        out_specs=ANY,
        name="to_pieces",
    )(rows.reshape(8, 16, WIDTH), *late)
    return pieces.reshape(RANKS, 16, 768)


def from_pieces(pieces, *late):
    def body(x_ref, out):
        for b in range(4):
            yield x_ref.at[:, b], out.at[:, :, pl.ds(768 * b, 768)]

    rows = copies(body, 4, 1, len(late))(
        out_shape=jax.ShapeDtypeStruct((8, 16, WIDTH), BF),
        in_specs=[ANY] + [ANY] * len(late),
        out_specs=ANY,
        name="from_pieces",
    )(pieces.reshape(PIECES), *late)
    return rows.reshape(ROWS, WIDTH)


def reorder(destinations, pieces, back, *late):
    def body(d_ref, x_ref, out):
        for c in range(RANKS):
            if back:
                yield x_ref.at[c], out.at[d_ref[c]]
            else:
                yield x_ref.at[d_ref[c]], out.at[c]

    return copies(body, RANKS, 2, len(late), 100)(
        out_shape=jax.ShapeDtypeStruct((RANKS, 16, 768), BF),
        in_specs=[SMEM, ANY] + [ANY] * len(late),
        out_specs=ANY,
        name="reorder",
    )(destinations, pieces, *late)


def split_cotangent(at, pieces, *late):
    def body(at_ref, x_ref, own, other):
        for k in range(CHIPS):
            chip, core = place(at_ref, k)
            for out, half in ((own, core), (other, 1 - core)):
                start = pl.multiple_of(half * GRP, GRP)
                yield x_ref.at[:, chip, :, pl.ds(start, GRP)], out.at[k]

    own, other = copies(body, 2 * CHIPS, 2, len(late))(
        out_shape=[jax.ShapeDtypeStruct((CHIPS, 8, 16, GRP), BF)] * 2,
        in_specs=[SMEM, ANY] + [ANY] * len(late),
        out_specs=[ANY] * 2,
        name="split_cotangent",
    )(at, pieces.reshape(PIECES), *late)
    return own.reshape(CHIPS, ROWS, GRP), other.reshape(CHIPS, ROWS, GRP)


def join_pieces(at, blocks, sibling, *late):
    def body(at_ref, *refs):
        out = refs[-1]
        for k in range(CHIPS):
            chip, core = place(at_ref, k)
            for src, half in ((refs[k].at[pl.ds(0, 8)], core), (refs[CHIPS].at[k], 1 - core)):
                start = pl.multiple_of(half * GRP, GRP)
                yield src, out.at[:, chip, :, pl.ds(start, GRP)]

    pieces = copies(body, 2 * CHIPS, 2 + CHIPS, len(late))(
        out_shape=jax.ShapeDtypeStruct(PIECES, BF),
        in_specs=[SMEM] + [ANY] * (1 + CHIPS + len(late)),
        out_specs=ANY,
        name="join_pieces",
    )(at, *(b.reshape(16, 16, GRP) for b in blocks), sibling.reshape(CHIPS, 8, 16, GRP), *late)
    return pieces.reshape(RANKS, 16, 768)


def live_rows(at, lengths, text_lengths):
    row = lax.broadcasted_iota(jnp.int32, (SEQ, DH), 0)
    chip = lax.bitwise_and((at[0] >> 1) + CHIPS - lax.shift_right_logical(row, 8), CHIPS - 1)
    core = lax.bitwise_xor(at[0] & 1, lax.bitwise_and(lax.shift_right_logical(row, 7), 1))
    pos = (2 * chip + core) * ROWS + lax.bitwise_and(row, ROWS - 1)
    latent, text = lengths[at[1]], text_lengths[at[1]]
    return (pos < latent) | ((pos >= CAP) & (pos < CAP + text))


def cols(part, head):
    return pl.ds(part * GRP + head * DH, DH)


def moves(refs, held, sems, parts, inward):
    heads = []
    for g in range(MINE):
        out = []
        for k in range(CHIPS):
            for t in range(parts):
                block = refs[k].at[:, cols(t, g)]
                rows = held.at[pl.ds(k * CH, CH), cols(t, g)]
                src, dst = (block, rows) if inward else (rows, block)
                out.append(pltpu.make_async_copy(src, dst, sems.at[g, k, t]))
        heads.append(out)
    return heads


def begin(started):
    for cp in started:
        cp.start()


def finish(started):
    for cp in started:
        cp.wait()


def thirds(value):
    hi = value.astype(BF).astype(F32)
    mid = (value - hi).astype(BF).astype(F32)
    return hi, mid, value - hi - mid


def forward_kernel(at, lengths, text_lengths, *refs):
    xs = refs[:CHIPS]
    outs = refs[CHIPS : 2 * CHIPS]
    wide, norm, token, held, done, wide_held, in_sems, out_sems, wide_sems = refs[2 * CHIPS :]
    token[...] = jnp.zeros_like(token)

    arriving = moves(xs, held, in_sems, 3, True)
    leaving = moves(outs, done, out_sems, 1, False)
    for g in range(MINE):
        leaving[g].append(pltpu.make_async_copy(wide_held.at[g], wide.at[g], wide_sems.at[g]))
        begin(arriving[g])

    live = live_rows(at, lengths, text_lengths)
    lane = lax.broadcasted_iota(jnp.int32, (SEQ, DH), 1)
    dead = jnp.where(live | (lane > 0), 0.0, -1e30).astype(BF)
    unit = jnp.where(lane == 0, 1.0, 0.0).astype(BF)
    livef = live.astype(F32)
    for g in range(MINE):
        finish(arriving[g])

    def logits(g, n):
        rows = slice(n * CH, (n + 1) * CH)
        q = jnp.concatenate([held[rows, cols(0, g)], unit[rows]], axis=1)
        k = jnp.concatenate([held[:, cols(1, g)], dead], axis=1)
        return lax.dot_general(k, q, NT, preferred_element_type=F32)

    steps = [(g, n) for g in range(MINE) for n in range(SEQ // CH)]
    ahead = logits(*steps[0])
    for step, (g, n) in enumerate(steps):
        part = slice(n * CH, (n + 1) * CH)
        s = ahead
        if step + 1 < len(steps):
            ahead = logits(*steps[step + 1])
        if n == 0:
            vt = held[:, cols(2, g)].T
        top = jnp.max(s, axis=0, keepdims=True)
        e = jnp.exp2((s - top) * LOGIT)
        total = jnp.sum(e, axis=0, keepdims=True)
        norm[g, :, part] = top + jnp.log2(total) * (1.0 / LOGIT)
        p = e.astype(BF)
        rest = (e - p.astype(F32)).astype(BF)
        o = jnp.dot(vt, p, preferred_element_type=F32)
        o = o + jnp.dot(vt, rest, preferred_element_type=F32)
        o = (o * (1.0 / total)).T
        wide_held[g, part, :] = o
        done[part, cols(0, g)] = (o * livef[part]).astype(BF)
    for g in range(MINE):
        begin(leaving[g])
    for g in range(MINE):
        finish(leaving[g])


def backward_kernel(at, lengths, text_lengths, *refs):
    xs = refs[:CHIPS]
    cs = refs[CHIPS : 2 * CHIPS]
    wide, norm = refs[2 * CHIPS : 2 * CHIPS + 2]
    outs = refs[2 * CHIPS + 2 : 3 * CHIPS + 2]
    token, held, cot, done, dst, pst, wide_held, in_sems, cot_sems, out_sems, wide_sems = refs[3 * CHIPS + 2 :]

    arriving = moves(xs, held, in_sems, 3, True)
    coming = moves(cs, cot, cot_sems, 1, True)
    leaving = moves(outs, done, out_sems, 3, False)
    for g in range(MINE):
        arriving[g].append(pltpu.make_async_copy(wide.at[g], wide_held.at[g], wide_sems.at[g]))
        begin(arriving[g] + coming[g])
    token[...] = jnp.zeros_like(token)

    live = live_rows(at, lengths, text_lengths)
    lane = lax.broadcasted_iota(jnp.int32, (SEQ, DH), 1)
    units = jnp.where(lane < 3, 1.0, 0.0).astype(BF)
    dead = jnp.where(lane < 3, 1.0, jnp.where(live | (lane > 3), 0.0, -1e30)).astype(BF)

    def three(value, rest):
        hi, mid, low = thirds(value)
        low = jnp.where(lane == 2, -low, rest)
        return jnp.where(lane == 0, -hi, jnp.where(lane == 1, -mid, low)).astype(BF)

    one = jnp.where(lane == 3, 1.0, 0.0)
    for g in range(MINE):
        finish(arriving[g] + coming[g])

    def masked(g):
        return jnp.where(live, cot[:, cols(0, g)], jnp.zeros((), BF))

    def key_value(g, n):
        part = slice(n * IC, (n + 1) * IC)
        slot = g % 2
        dk = jnp.dot(dst[slot, part, :], held[:, cols(0, g)], preferred_element_type=F32) * SCALE
        done[part, cols(1, g)] = dk.astype(BF)
        dv = jnp.dot(pst[slot, part, :], masked(g), preferred_element_type=F32)
        done[part, cols(2, g)] = dv.astype(BF)

    for g in range(MINE):
        do = masked(g)
        dot = jnp.sum(do.astype(F32) * wide_held[g], axis=1, keepdims=True)
        dox = jnp.concatenate([do, three(dot, 0.0)], axis=1)
        vx = jnp.concatenate([held[:, cols(2, g)], units], axis=1)
        qx = jnp.concatenate([held[:, cols(0, g)], three(norm[g].T, one)], axis=1)
        kx = jnp.concatenate([held[:, cols(1, g)], dead], axis=1)
        kt = held[:, cols(1, g)].T
        for n in range(SEQ // IC):
            part = slice(n * IC, (n + 1) * IC)
            s = lax.dot_general(kx, qx[part], NT, preferred_element_type=F32)
            dp = lax.dot_general(vx, dox[part], NT, preferred_element_type=F32)
            p = jnp.exp2(s * LOGIT)
            pst[g % 2, :, part] = p.astype(BF)
            ds = (p * dp).astype(BF)
            dst[g % 2, :, part] = ds
            dq = jnp.dot(kt, ds, preferred_element_type=F32).T * SCALE
            done[part, cols(0, g)] = dq.astype(BF)
        for n in range(SEQ // IC):
            key_value(g, n)
    for g in range(MINE):
        begin(leaving[g])
    for g in range(MINE):
        finish(leaving[g])


NORM = pl.BlockSpec((MINE, 1, SEQ), lambda g: (0, 0, 0))


def forward(where, xs):
    return pl.pallas_call(
        forward_kernel,
        grid=(1,),
        out_shape=[jax.ShapeDtypeStruct((CH, GRP), BF)] * CHIPS
        + [pltpu.HBM((MINE, SEQ, DH), F32), pltpu.HBM((MINE, 1, SEQ), F32), TOKEN],
        in_specs=[SMEM] * 3 + [ANY] * CHIPS,
        out_specs=[ANY] * (CHIPS + 1) + [NORM, pl.BlockSpec((8, 128), lambda g: (0, 0))],
        scratch_shapes=[
            pltpu.VMEM((SEQ, 3 * GRP), BF),
            pltpu.VMEM((SEQ, GRP), BF),
            pltpu.VMEM((MINE, SEQ, DH), F32),
            pltpu.SemaphoreType.DMA((MINE, CHIPS, 3)),
            pltpu.SemaphoreType.DMA((MINE, CHIPS, 1)),
            pltpu.SemaphoreType.DMA((MINE,)),
        ],
        compiler_params=pltpu.CompilerParams(vmem_limit_bytes=FWD_VMEM << 20),
        cost_estimate=pl.CostEstimate(
            flops=20 * MINE * 2 * 5 * SEQ * SEQ * DH, bytes_accessed=12 << 20, transcendentals=MINE * SEQ * SEQ
        ),
        name="attend",
    )(*where, *xs)


def backward(where, cs, xs, wide, norm):
    return pl.pallas_call(
        backward_kernel,
        grid=(1,),
        out_shape=[jax.ShapeDtypeStruct((CH, 3 * GRP), BF)] * CHIPS + [TOKEN],
        in_specs=[SMEM] * 3 + [ANY] * (2 * CHIPS) + [ANY, NORM],
        out_specs=[ANY] * CHIPS + [pl.BlockSpec((8, 128), lambda g: (0, 0))],
        scratch_shapes=[
            pltpu.VMEM((SEQ, 3 * GRP), BF),
            pltpu.VMEM((SEQ, GRP), BF),
            pltpu.VMEM((SEQ, 3 * GRP), BF),
            pltpu.VMEM((2, SEQ, SEQ), BF),
            pltpu.VMEM((2, SEQ, SEQ), BF),
            pltpu.VMEM((MINE, SEQ, DH), F32),
            pltpu.SemaphoreType.DMA((MINE, CHIPS, 3)),
            pltpu.SemaphoreType.DMA((MINE, CHIPS, 1)),
            pltpu.SemaphoreType.DMA((MINE, CHIPS, 3)),
            pltpu.SemaphoreType.DMA((MINE,)),
        ],
        compiler_params=pltpu.CompilerParams(vmem_limit_bytes=BWD_VMEM << 20),
        cost_estimate=pl.CostEstimate(
            flops=20 * MINE * 2 * 8 * SEQ * SEQ * DH, bytes_accessed=16 << 20, transcendentals=0
        ),
        name="attend_grad",
    )(*where, *xs, *cs, wide, norm)


def turn(blocks, sign):
    out = [blocks[0]]
    for k in range(1, CHIPS):
        pairs = [(s, (s + sign * 2 * k) % SHARDS) for s in range(SHARDS)]
        out.append(lax.ppermute(blocks[k], "seq", pairs))
    return out


def swap(block):
    return lax.ppermute(block, "seq", [(s, s ^ 1) for s in range(SHARDS)])


def spread(pieces):
    return lax.all_to_all(pieces, "dp", split_axis=0, concat_axis=0, tiled=True)


def on_device(projected, cotangent, lengths, text_lengths, destinations):
    me = lax.axis_index("seq").astype(jnp.int32)
    at = jnp.stack([me, lax.axis_index("dp").astype(jnp.int32)])
    where = (at, lengths, text_lengths)

    own, other = split_projected(at, projected[0])
    *xs, paired = pair(own, swap(other))
    xs = turn(xs, 1)
    there = spread(to_pieces(cotangent[0]))
    here = spread(reorder(destinations, there, False, paired))

    *outs, wide, norm, attended_once = forward(where, xs)
    os = turn(outs, -1)
    own, other = split_cotangent(at, here, attended_once)
    *cs, paired = pair(own, swap(other))
    halfway = spread(join_pieces(at, os, swap(for_sibling(os)), paired))
    cs = turn(cs, 1)

    *gs, graded = backward(where, cs, xs, wide, norm)
    gs = turn(gs, -1)
    home = spread(reorder(destinations, halfway, True, graded))
    sibling = for_sibling(gs)
    projected_grad = join_gradient(at, gs, True, (), sibling)
    projected_grad = join_gradient(at, (swap(sibling),), False, (projected_grad,))
    attended = from_pieces(home)
    return attended[None], projected_grad[None]


def solution(mesh):
    in_specs = (P("dp", "seq", None), P("dp", "seq", None), P(), P(), P())
    out_specs = (P("dp", "seq", None), P("dp", "seq", None))
    return jax.shard_map(
        on_device, mesh=mesh, in_specs=in_specs, out_specs=out_specs, check_vma=False
    )
```

```python
import functools
import jax
import jax.numpy as jnp
from jax import lax
from jax.experimental import pallas as pl
from jax.experimental.pallas import tpu as pltpu
from jax.sharding import PartitionSpec as P

HEADS = 24
DH = 128
CAP = 512
SEQ = 1024
RANKS = 32
SHARDS = 8
ROWS = SEQ // SHARDS
MINE = HEADS // SHARDS
GRP = MINE * DH
WIDTH = HEADS * DH
CHIPS = SHARDS // 2
PIECES = (8, 4, 16, 768)
IC = 512
CH = 2 * ROWS
SCALE = DH ** -0.5
LOGIT = SCALE * 1.4426950408889634
FWD_VMEM = 24
BWD_VMEM = 32
NT = (((1,), (1,)), ((), ()))

ANY = pl.BlockSpec(memory_space=pl.ANY)
SMEM = pl.BlockSpec(memory_space=pltpu.SMEM)
VMEM = pl.BlockSpec(memory_space=pltpu.VMEM)
BF = jnp.bfloat16
F32 = jnp.float32
TOKEN = jax.ShapeDtypeStruct((8, 128), F32)


def copies(body, count, given, late, cost=4):
    def kernel(*refs):
        sems = refs[-1]
        started = []
        used = refs[:given] + refs[given + late : -1]
        for n, (src, dst) in enumerate(body(*used)):
            cp = pltpu.make_async_copy(src, dst, sems.at[n])
            cp.start()
            started.append(cp)
        for cp in started:
            cp.wait()

    return functools.partial(
        pl.pallas_call,
        kernel,
        scratch_shapes=[pltpu.SemaphoreType.DMA((count,))],
        compiler_params=pltpu.CompilerParams(vmem_limit_bytes=1 << 20),
        cost_estimate=pl.CostEstimate(flops=0, bytes_accessed=cost << 20, transcendentals=0),
    )


def place(at, k):
    return lax.bitwise_and(lax.shift_right_logical(at[0], 1) + k, CHIPS - 1), at[0] & 1


def split_kernel(at, x_ref, own, other, mine, theirs, in_sems, out_sems):
    arriving, leaving = [], []
    for k in range(CHIPS):
        chip, core = place(at, k)
        for side, (held, head) in enumerate(((theirs, 2 * chip + 1 - core), (mine, 2 * chip + core))):
            group = []
            for t in range(3):
                start = pl.multiple_of(t * WIDTH + head * GRP, GRP)
                src = x_ref.at[:, pl.ds(start, GRP)]
                dst = held.at[k, :, pl.ds(t * GRP, GRP)]
                group.append(pltpu.make_async_copy(src, dst, in_sems.at[k, side, t]))
            arriving.append(group)
            out = (other, own)[side].at[k]
            leaving.append(pltpu.make_async_copy(held.at[k], out, out_sems.at[k, side]))
    for group in arriving:
        begin(group)
    for group, cp in zip(arriving, leaving):
        finish(group)
        cp.start()
    finish(leaving)


def split_projected(at, projected):
    return pl.pallas_call(
        split_kernel,
        out_shape=[pltpu.HBM((CHIPS, ROWS, 3 * GRP), BF)] * 2,
        in_specs=[SMEM, ANY],
        out_specs=[ANY] * 2,
        scratch_shapes=[
            pltpu.VMEM((CHIPS, ROWS, 3 * GRP), BF),
            pltpu.VMEM((CHIPS, ROWS, 3 * GRP), BF),
            pltpu.SemaphoreType.DMA((CHIPS, 2, 3)),
            pltpu.SemaphoreType.DMA((CHIPS, 2)),
        ],
        compiler_params=pltpu.CompilerParams(vmem_limit_bytes=62 << 20),
        cost_estimate=pl.CostEstimate(flops=0, bytes_accessed=4 << 20, transcendentals=0),
        name="split_projected",
    )(at, projected)


def join_gradient(at, parts, own, so_far, *late):
    def body(at_ref, *refs):
        out = refs[-1]
        for k in range(CHIPS):
            chip, core = place(at_ref, k)
            src = refs[k].at[pl.ds(0, ROWS)] if own else refs[0].at[k]
            head = 2 * chip + (core if own else 1 - core)
            for t in range(3):
                start = pl.multiple_of(t * WIDTH + head * GRP, GRP)
                yield src.at[:, pl.ds(t * GRP, GRP)], out.at[:, pl.ds(start, GRP)]

    given = (at, *parts, *so_far)
    return copies(body, 3 * CHIPS, len(given), len(late))(
        out_shape=pltpu.HBM((ROWS, 3 * WIDTH), BF),
        in_specs=[SMEM] + [ANY] * (len(given) - 1 + len(late)),
        out_specs=ANY,
        input_output_aliases={} if own else {2: 0},
        name="join_gradient",
    )(*given, *late)


def pair(own, recv, *late):
    width = own.shape[2]

    def body(own_ref, recv_ref, *outs):
        outs[CHIPS][...] = jnp.zeros_like(outs[CHIPS])
        for k in range(CHIPS):
            yield own_ref.at[k], outs[k].at[pl.ds(0, ROWS)]
            yield recv_ref.at[k], outs[k].at[pl.ds(ROWS, ROWS)]

    return copies(body, 2 * CHIPS, 2, len(late))(
        out_shape=[pltpu.HBM((2 * ROWS, width), BF)] * CHIPS
        + [TOKEN],
        in_specs=[ANY] * (2 + len(late)),
        out_specs=[ANY] * CHIPS + [VMEM],
        name="pair",
    )(own, recv, *late)


def for_sibling(blocks, *late):
    width = blocks[0].shape[1]

    def body(*refs):
        for k in range(CHIPS):
            yield refs[k].at[pl.ds(ROWS, ROWS)], refs[CHIPS].at[k]

    return copies(body, CHIPS, CHIPS, len(late))(
        out_shape=jax.ShapeDtypeStruct((CHIPS, ROWS, width), BF),
        in_specs=[ANY] * (CHIPS + len(late)),
        out_specs=ANY,
        name="for_sibling",
    )(*blocks, *late)


def to_pieces(rows, *late):
    def body(x_ref, out):
        for b in range(4):
            yield x_ref.at[:, :, pl.ds(768 * b, 768)], out.at[:, b]

    pieces = copies(body, 4, 1, len(late))(
        out_shape=jax.ShapeDtypeStruct(PIECES, BF),
        in_specs=[ANY] + [ANY] * len(late),
        out_specs=ANY,
        name="to_pieces",
    )(rows.reshape(8, 16, WIDTH), *late)
    return pieces.reshape(RANKS, 16, 768)


def from_pieces(pieces, *late):
    def body(x_ref, out):
        for b in range(4):
            yield x_ref.at[:, b], out.at[:, :, pl.ds(768 * b, 768)]

    rows = copies(body, 4, 1, len(late))(
        out_shape=jax.ShapeDtypeStruct((8, 16, WIDTH), BF),
        in_specs=[ANY] + [ANY] * len(late),
        out_specs=ANY,
        name="from_pieces",
    )(pieces.reshape(PIECES), *late)
    return rows.reshape(ROWS, WIDTH)


def reorder(destinations, pieces, back, *late):
    def body(d_ref, x_ref, out):
        for c in range(RANKS):
            if back:
                yield x_ref.at[c], out.at[d_ref[c]]
            else:
                yield x_ref.at[d_ref[c]], out.at[c]

    return copies(body, RANKS, 2, len(late), 100)(
        out_shape=jax.ShapeDtypeStruct((RANKS, 16, 768), BF),
        in_specs=[SMEM, ANY] + [ANY] * len(late),
        out_specs=ANY,
        name="reorder",
    )(destinations, pieces, *late)


def split_cotangent(at, pieces, *late):
    def body(at_ref, x_ref, own, other):
        for k in range(CHIPS):
            chip, core = place(at_ref, k)
            for out, half in ((own, core), (other, 1 - core)):
                start = pl.multiple_of(half * GRP, GRP)
                yield x_ref.at[:, chip, :, pl.ds(start, GRP)], out.at[k]

    own, other = copies(body, 2 * CHIPS, 2, len(late))(
        out_shape=[jax.ShapeDtypeStruct((CHIPS, 8, 16, GRP), BF)] * 2,
        in_specs=[SMEM, ANY] + [ANY] * len(late),
        out_specs=[ANY] * 2,
        name="split_cotangent",
    )(at, pieces.reshape(PIECES), *late)
    return own.reshape(CHIPS, ROWS, GRP), other.reshape(CHIPS, ROWS, GRP)


def join_pieces(at, blocks, sibling, *late):
    def body(at_ref, *refs):
        out = refs[-1]
        for k in range(CHIPS):
            chip, core = place(at_ref, k)
            for src, half in ((refs[k].at[pl.ds(0, 8)], core), (refs[CHIPS].at[k], 1 - core)):
                start = pl.multiple_of(half * GRP, GRP)
                yield src, out.at[:, chip, :, pl.ds(start, GRP)]

    pieces = copies(body, 2 * CHIPS, 2 + CHIPS, len(late))(
        out_shape=jax.ShapeDtypeStruct(PIECES, BF),
        in_specs=[SMEM] + [ANY] * (1 + CHIPS + len(late)),
        out_specs=ANY,
        name="join_pieces",
    )(at, *(b.reshape(16, 16, GRP) for b in blocks), sibling.reshape(CHIPS, 8, 16, GRP), *late)
    return pieces.reshape(RANKS, 16, 768)


def live_rows(at, lengths, text_lengths):
    row = lax.broadcasted_iota(jnp.int32, (SEQ, DH), 0)
    chip = lax.bitwise_and((at[0] >> 1) + CHIPS - lax.shift_right_logical(row, 8), CHIPS - 1)
    core = lax.bitwise_xor(at[0] & 1, lax.bitwise_and(lax.shift_right_logical(row, 7), 1))
    pos = (2 * chip + core) * ROWS + lax.bitwise_and(row, ROWS - 1)
    latent, text = lengths[at[1]], text_lengths[at[1]]
    return (pos < latent) | ((pos >= CAP) & (pos < CAP + text))


def cols(part, head):
    return pl.ds(part * GRP + head * DH, DH)


def moves(refs, held, sems, parts, inward):
    heads = []
    for g in range(MINE):
        out = []
        for k in range(CHIPS):
            for t in range(parts):
                block = refs[k].at[:, cols(t, g)]
                rows = held.at[pl.ds(k * CH, CH), cols(t, g)]
                src, dst = (block, rows) if inward else (rows, block)
                out.append(pltpu.make_async_copy(src, dst, sems.at[g, k, t]))
        heads.append(out)
    return heads


def begin(started):
    for cp in started:
        cp.start()


def finish(started):
    for cp in started:
        cp.wait()


def thirds(value):
    hi = value.astype(BF).astype(F32)
    mid = (value - hi).astype(BF).astype(F32)
    return hi, mid, value - hi - mid


def forward_kernel(at, lengths, text_lengths, *refs):
    xs = refs[:CHIPS]
    outs = refs[CHIPS : 2 * CHIPS]
    wide, norm, token, held, done, wide_held, in_sems, out_sems, wide_sems = refs[2 * CHIPS :]
    token[...] = jnp.zeros_like(token)

    arriving = moves(xs, held, in_sems, 3, True)
    leaving = moves(outs, done, out_sems, 1, False)
    for g in range(MINE):
        leaving[g].append(pltpu.make_async_copy(wide_held.at[g], wide.at[g], wide_sems.at[g]))
        begin(arriving[g])

    live = live_rows(at, lengths, text_lengths)
    lane = lax.broadcasted_iota(jnp.int32, (SEQ, DH), 1)
    dead = jnp.where(live | (lane > 0), 0.0, -1e30).astype(BF)
    unit = jnp.where(lane == 0, 1.0, 0.0).astype(BF)
    livef = live.astype(F32)
    for g in range(MINE):
        finish(arriving[g])

    def logits(g, n):
        rows = slice(n * CH, (n + 1) * CH)
        q = jnp.concatenate([held[rows, cols(0, g)], unit[rows]], axis=1)
        k = jnp.concatenate([held[:, cols(1, g)], dead], axis=1)
        return lax.dot_general(k, q, NT, preferred_element_type=F32)

    steps = [(g, n) for g in range(MINE) for n in range(SEQ // CH)]
    ahead = logits(*steps[0])
    for step, (g, n) in enumerate(steps):
        part = slice(n * CH, (n + 1) * CH)
        s = ahead
        if step + 1 < len(steps):
            ahead = logits(*steps[step + 1])
        if n == 0:
            vt = held[:, cols(2, g)].T
        top = jnp.max(s, axis=0, keepdims=True)
        e = jnp.exp2((s - top) * LOGIT)
        total = jnp.sum(e, axis=0, keepdims=True)
        norm[g, :, part] = top + jnp.log2(total) * (1.0 / LOGIT)
        p = e.astype(BF)
        rest = (e - p.astype(F32)).astype(BF)
        o = jnp.dot(vt, p, preferred_element_type=F32)
        o = o + jnp.dot(vt, rest, preferred_element_type=F32)
        o = (o * (1.0 / total)).T
        wide_held[g, part, :] = o
        done[part, cols(0, g)] = (o * livef[part]).astype(BF)
    for g in range(MINE):
        begin(leaving[g])
    for g in range(MINE):
        finish(leaving[g])


def backward_kernel(at, lengths, text_lengths, *refs):
    xs = refs[:CHIPS]
    cs = refs[CHIPS : 2 * CHIPS]
    wide, norm = refs[2 * CHIPS : 2 * CHIPS + 2]
    outs = refs[2 * CHIPS + 2 : 3 * CHIPS + 2]
    token, held, cot, done, dst, pst, wide_held, in_sems, cot_sems, out_sems, wide_sems = refs[3 * CHIPS + 2 :]

    arriving = moves(xs, held, in_sems, 3, True)
    coming = moves(cs, cot, cot_sems, 1, True)
    leaving = moves(outs, done, out_sems, 3, False)
    for g in range(MINE):
        arriving[g].append(pltpu.make_async_copy(wide.at[g], wide_held.at[g], wide_sems.at[g]))
        begin(arriving[g] + coming[g])
    token[...] = jnp.zeros_like(token)

    live = live_rows(at, lengths, text_lengths)
    lane = lax.broadcasted_iota(jnp.int32, (SEQ, DH), 1)
    units = jnp.where(lane < 3, 1.0, 0.0).astype(BF)
    dead = jnp.where(lane < 3, 1.0, jnp.where(live | (lane > 3), 0.0, -1e30)).astype(BF)

    def three(value, rest):
        hi, mid, low = thirds(value)
        low = jnp.where(lane == 2, -low, rest)
        return jnp.where(lane == 0, -hi, jnp.where(lane == 1, -mid, low)).astype(BF)

    one = jnp.where(lane == 3, 1.0, 0.0)
    for g in range(MINE):
        finish(arriving[g] + coming[g])

    def masked(g):
        return jnp.where(live, cot[:, cols(0, g)], jnp.zeros((), BF))

    def key_value(g, n):
        part = slice(n * IC, (n + 1) * IC)
        slot = g % 2
        dk = jnp.dot(dst[slot, part, :], held[:, cols(0, g)], preferred_element_type=F32) * SCALE
        done[part, cols(1, g)] = dk.astype(BF)
        dv = jnp.dot(pst[slot, part, :], masked(g), preferred_element_type=F32)
        done[part, cols(2, g)] = dv.astype(BF)

    for g in range(MINE):
        do = masked(g)
        dot = jnp.sum(do.astype(F32) * wide_held[g], axis=1, keepdims=True)
        dox = jnp.concatenate([do, three(dot, 0.0)], axis=1)
        vx = jnp.concatenate([held[:, cols(2, g)], units], axis=1)
        qx = jnp.concatenate([held[:, cols(0, g)], three(norm[g].T, one)], axis=1)
        kx = jnp.concatenate([held[:, cols(1, g)], dead], axis=1)
        kt = held[:, cols(1, g)].T
        for n in range(SEQ // IC):
            part = slice(n * IC, (n + 1) * IC)
            s = lax.dot_general(kx, qx[part], NT, preferred_element_type=F32)
            dp = lax.dot_general(vx, dox[part], NT, preferred_element_type=F32)
            p = jnp.exp2(s * LOGIT)
            pst[g % 2, :, part] = p.astype(BF)
            ds = (p * dp).astype(BF)
            dst[g % 2, :, part] = ds
            dq = jnp.dot(kt, ds, preferred_element_type=F32).T * SCALE
            done[part, cols(0, g)] = dq.astype(BF)
        for n in range(SEQ // IC):
            key_value(g, n)
    for g in range(MINE):
        begin(leaving[g])
    for g in range(MINE):
        finish(leaving[g])


NORM = pl.BlockSpec((MINE, 1, SEQ), lambda g: (0, 0, 0))


def forward(where, xs):
    return pl.pallas_call(
        forward_kernel,
        grid=(1,),
        out_shape=[jax.ShapeDtypeStruct((CH, GRP), BF)] * CHIPS
        + [pltpu.HBM((MINE, SEQ, DH), F32), pltpu.HBM((MINE, 1, SEQ), F32), TOKEN],
        in_specs=[SMEM] * 3 + [ANY] * CHIPS,
        out_specs=[ANY] * (CHIPS + 1) + [NORM, pl.BlockSpec((8, 128), lambda g: (0, 0))],
        scratch_shapes=[
            pltpu.VMEM((SEQ, 3 * GRP), BF),
            pltpu.VMEM((SEQ, GRP), BF),
            pltpu.VMEM((MINE, SEQ, DH), F32),
            pltpu.SemaphoreType.DMA((MINE, CHIPS, 3)),
            pltpu.SemaphoreType.DMA((MINE, CHIPS, 1)),
            pltpu.SemaphoreType.DMA((MINE,)),
        ],
        compiler_params=pltpu.CompilerParams(vmem_limit_bytes=FWD_VMEM << 20),
        cost_estimate=pl.CostEstimate(
            flops=20 * MINE * 2 * 5 * SEQ * SEQ * DH, bytes_accessed=12 << 20, transcendentals=MINE * SEQ * SEQ
        ),
        name="attend",
    )(*where, *xs)


def backward(where, cs, xs, wide, norm):
    return pl.pallas_call(
        backward_kernel,
        grid=(1,),
        out_shape=[jax.ShapeDtypeStruct((CH, 3 * GRP), BF)] * CHIPS + [TOKEN],
        in_specs=[SMEM] * 3 + [ANY] * (2 * CHIPS) + [ANY, NORM],
        out_specs=[ANY] * CHIPS + [pl.BlockSpec((8, 128), lambda g: (0, 0))],
        scratch_shapes=[
            pltpu.VMEM((SEQ, 3 * GRP), BF),
            pltpu.VMEM((SEQ, GRP), BF),
            pltpu.VMEM((SEQ, 3 * GRP), BF),
            pltpu.VMEM((2, SEQ, SEQ), BF),
            pltpu.VMEM((2, SEQ, SEQ), BF),
            pltpu.VMEM((MINE, SEQ, DH), F32),
            pltpu.SemaphoreType.DMA((MINE, CHIPS, 3)),
            pltpu.SemaphoreType.DMA((MINE, CHIPS, 1)),
            pltpu.SemaphoreType.DMA((MINE, CHIPS, 3)),
            pltpu.SemaphoreType.DMA((MINE,)),
        ],
        compiler_params=pltpu.CompilerParams(vmem_limit_bytes=BWD_VMEM << 20),
        cost_estimate=pl.CostEstimate(
            flops=20 * MINE * 2 * 8 * SEQ * SEQ * DH, bytes_accessed=16 << 20, transcendentals=0
        ),
        name="attend_grad",
    )(*where, *xs, *cs, wide, norm)


def turn(blocks, sign):
    out = [blocks[0]]
    for k in range(1, CHIPS):
        pairs = [(s, (s + sign * 2 * k) % SHARDS) for s in range(SHARDS)]
        out.append(lax.ppermute(blocks[k], "seq", pairs))
    return out


def swap(block):
    return lax.ppermute(block, "seq", [(s, s ^ 1) for s in range(SHARDS)])


def spread(pieces):
    return lax.all_to_all(pieces, "dp", split_axis=0, concat_axis=0, tiled=True)


def on_device(projected, cotangent, lengths, text_lengths, destinations):
    me = lax.axis_index("seq").astype(jnp.int32)
    at = jnp.stack([me, lax.axis_index("dp").astype(jnp.int32)])
    where = (at, lengths, text_lengths)

    own, other = split_projected(at, projected[0])
    *xs, paired = pair(own, swap(other))
    xs = turn(xs, 1)
    there = spread(to_pieces(cotangent[0]))
    here = spread(reorder(destinations, there, False, paired))

    *outs, wide, norm, attended_once = forward(where, xs)
    os = turn(outs, -1)
    own, other = split_cotangent(at, here, attended_once)
    *cs, paired = pair(own, swap(other))
    halfway = spread(join_pieces(at, os, swap(for_sibling(os)), paired))
    cs = turn(cs, 1)

    *gs, graded = backward(where, cs, xs, wide, norm)
    gs = turn(gs, -1)
    home = spread(reorder(destinations, halfway, True, graded))
    sibling = for_sibling(gs)
    projected_grad = join_gradient(at, gs, True, (), sibling)
    projected_grad = join_gradient(at, (swap(sibling),), False, (projected_grad,))
    attended = from_pieces(home)
    return attended[None], projected_grad[None]


def solution(mesh):
    in_specs = (P("dp", "seq", None), P("dp", "seq", None), P(), P(), P())
    out_specs = (P("dp", "seq", None), P("dp", "seq", None))
    return jax.shard_map(
        on_device, mesh=mesh, in_specs=in_specs, out_specs=out_specs, check_vma=False
    )
```
